32 devices in a mesh: dp: 16 (over z, y, core), opt: 2 (over x).
Axes of the slice: x: 2, y: 2, z: 4, core: 2. Of those that a mesh axis runs over, the one named last changes fastest.
Arguments:
- tokens: bfloat16 [16384, 384], P(('dp', 'opt')), may hold values from -6 to 6
- segment: int32 [16384], P(('dp', 'opt')), may hold values from -1 to 3, as said below
- cotangent: bfloat16 [16384, 384], P(('dp', 'opt')), may hold values from -6 to 6
- w_attn: float32 [384, 1536], P('opt'), may hold values from -0.4375 to 0.4375
- m_attn: float32 [384, 1536], P('opt'), may hold values from -28 to 28
- v_attn: float32 [384, 1536], P('opt'), may hold values from 81.92 to 327.68
- w_mlp: float32 [384, 3072], P('opt'), may hold values from -0.3125 to 0.3125
- m_mlp: float32 [384, 3072], P('opt'), may hold values from -32 to 32
- v_mlp: float32 [384, 3072], P('opt'), may hold values from 106.496 to 425.984
- vectors: float32 [4608], P('opt'), may hold values from -0.5 to 1.5, as said below
- m_vec: float32 [4608], P('opt'), may hold values from -32 to 32
- v_vec: float32 [4608], P('opt'), may hold values from 131.072 to 524.288
Outputs:
- activations: bfloat16 [16384, 384], P(('dp', 'opt'))
- input_grad: float32 [16384, 384], P(('dp', 'opt'))
- new_attn: float32 [384, 1536], P('opt')
- first_attn: float32 [384, 1536], P('opt')
- second_attn: float32 [384, 1536], P('opt')
- new_mlp: float32 [384, 3072], P('opt')
- first_mlp: float32 [384, 3072], P('opt')
- second_mlp: float32 [384, 3072], P('opt')
- new_vec: float32 [4608], P('opt')
- first_vec: float32 [4608], P('opt')
- second_vec: float32 [4608], P('opt')
The draws below stay inside these ranges and needn't reach their ends.
Inputs may be any that keep to these rules, and one draw needn't show every extreme that they name: `segment`: each device's 512 slots hold documents in order, numbered 0, 1, 2 and so on within the device, followed by empty slots marked -1; at least 128 slots of a device are live, and some device has all live. A document has 128 to 512 slots (the last live one of a device may have fewer), and some document has exactly 512. `vectors`: the entries of g1 and g2 lie in 0.5 to 1.5, all other entries in -0.5 to 0.5.
All inputs are finite; a program needn't handle non-finite values.
Results may differ from the reference program's by a relative error of at most 0.0095.
The reference program's roundings to bfloat16 on the way count: a program that leaves them out, or rounds other values in their place, can miss the bound.
Values may be sent and summed in bfloat16 or wider, within the bound.
No kernel may reach another device: no remote copies, remote signals or barrier semaphores. Data moves between devices by JAX's collectives and lax.ppermute only.
A program may use at most 128 MiB of HBM per device.

```python
import math
import jax
import jax.numpy as jnp
from jax import lax

D = 384
HEADS = 6
HEAD_DIM = 64
FF = 1536
TOK_DEV = 512
MAXLEN = 512
STEP = 10
TOKENS = 16384
VEC = 4608


def draw_segment(key, part):
    key = jax.random.fold_in(key, 7)
    device_count = TOKENS // TOK_DEV
    short_len = MAXLEN // 4
    doc_slots = TOK_DEV // short_len + 1
    key_len, key_live, key_full = jax.random.split(key, 3)
    lengths = jax.random.randint(key_len, (device_count, doc_slots), short_len, MAXLEN + 1)
    full_device = jax.random.randint(key_full, (), 0, device_count)
    long_device = (full_device + 1) % device_count
    device_index = jnp.arange(device_count)
    lengths = jnp.where((device_index == full_device)[:, None], short_len, lengths)
    lengths = jnp.where((device_index == long_device)[:, None] & (jnp.arange(doc_slots)[None, :] == 0), MAXLEN, lengths)
    live_count = jax.random.randint(key_live, (device_count,), TOK_DEV // 4, TOK_DEV + 1)
    live_count = jnp.where((device_index == full_device) | (device_index == long_device), TOK_DEV, live_count)
    doc_ends = jnp.cumsum(lengths, axis=1)
    slot_index = jnp.arange(TOK_DEV)
    doc_ids = jnp.sum((doc_ends[:, None, :] <= slot_index[None, :, None]).astype(jnp.int32), axis=2)
    doc_ids = jnp.where(slot_index[None, :] < live_count[:, None], doc_ids, -1)
    return doc_ids.reshape(device_count * TOK_DEV).astype(jnp.int32)


def draw_vectors(key, part):
    key = jax.random.fold_in(key, 11)
    base_draw = jax.random.uniform(key, (8 * D + FF,), jnp.float32, -0.5, 0.5)
    entry_index = jnp.arange(8 * D + FF)
    is_gain = (entry_index < D) | (entry_index >= 5 * D) & (entry_index < 6 * D)
    return jnp.where(is_gain, 1.0 + base_draw, base_draw).astype(jnp.float32)


def block_scale(key, dims, cuts, smallest, high):
    gain = 1.0
    for axis_at, blocks in cuts:
        steps = jax.random.uniform(jax.random.fold_in(jax.random.fold_in(key, 6), axis_at), (blocks,), jnp.float32, smallest / len(cuts), high / len(cuts))
        gain = gain * jnp.repeat(jnp.exp(steps), dims[axis_at] // blocks).reshape((-1,) + (1,) * (len(dims) - 1 - axis_at))
    return gain


def normal_values(key, shape, scale, bound, cuts=(), kind=jnp.bfloat16):
    factor_of = block_scale(key, shape, cuts, -0.22, 0.18) if cuts else 1.0
    drawn = jax.random.normal(key, shape, jnp.float32) * scale * factor_of
    return jnp.minimum(jnp.maximum(drawn, -bound), bound).astype(kind)


def setup_inputs(seed: int = 0) -> dict:
    key_of = jax.random.split(jax.random.key(seed), 13)
    return {
        "tokens": normal_values(key_of[0], (TOKENS, D), 1.0, 6.0, ((0, 32),)),
        "segment": draw_segment(jax.random.fold_in(key_of[12], 71), 0),
        "cotangent": normal_values(key_of[2], (TOKENS, D), 1.0, 6.0, ((0, 32),)),
        "w_attn": normal_values(key_of[3], (D, 4 * D), (D // 2) ** -0.5, 0.4375, ((0, 2),), jnp.float32),
        "m_attn": normal_values(key_of[4], (D, 4 * D), (0.035 * TOKENS ** 0.5), 28.0, ((0, 2),), jnp.float32),
        "v_attn": jnp.clip(jnp.exp(math.log(327.68) - 1.3862944 * jax.random.uniform(key_of[5], (D, 4 * D), jnp.float32) ** block_scale(key_of[5], (D, 4 * D), ((0, 2),), -0.2, 0.2)), 81.92, 327.68),
        "w_mlp": normal_values(key_of[6], (D, 2 * FF), D ** -0.5, 0.3125, ((0, 2),), jnp.float32),
        "m_mlp": normal_values(key_of[7], (D, 2 * FF), (0.04 * TOKENS ** 0.5), 32.0, ((0, 2),), jnp.float32),
        "v_mlp": jnp.clip(jnp.exp(math.log(425.984) - 1.3862944 * jax.random.uniform(key_of[8], (D, 2 * FF), jnp.float32) ** block_scale(key_of[8], (D, 2 * FF), ((0, 2),), -0.2, 0.2)), 106.496, 425.984),
        "vectors": draw_vectors(jax.random.fold_in(key_of[12], 71), 0),
        "m_vec": normal_values(key_of[10], (VEC,), (0.044 * TOKENS ** 0.5), 32.0, ((0, 2),), jnp.float32),
        "v_vec": jnp.clip(jnp.exp(math.log(524.288) - 1.3862944 * jax.random.uniform(key_of[11], (VEC,), jnp.float32) ** block_scale(key_of[11], (VEC,), ((0, 2),), -0.2, 0.2)), 131.072, 524.288),
    }


@jax.custom_vjp
def low(v):
    return lax.optimization_barrier(v.astype(jnp.bfloat16)).astype(jnp.float32)

@jax.custom_vjp
def low_back(v):
    return v

def low_keep(v):
    return (low(v), None)

def low_pass(kept, grad):
    return (grad,)

def back_keep(v):
    return (v, None)

def back_low(kept, grad):
    return (low(grad),)
low.defvjp(low_keep, low_pass)
low_back.defvjp(back_keep, back_low)
norm_eps = 1e-05
beta_one = 0.9
beta_two = 0.95
adam_eps = 1e-08
matrix_rate = 0.15
vector_rate = 0.6
matrix_decay = 0.1
neg_large = -1e+30
highest = lax.Precision.HIGHEST

def normalize(values, gain_vec, shift_vec):
    row_mean = lax.optimization_barrier(jnp.mean(values, axis=-1, keepdims=True))
    centred = values - row_mean
    variance = lax.optimization_barrier(jnp.mean(centred * centred, axis=-1, keepdims=True))
    return centred * lax.rsqrt(variance + norm_eps) * gain_vec + shift_vec

def gelu_tanh(values):
    return jax.nn.gelu(values, approximate=True)

def permitted(seg_query, seg_key, pos_query, pos_key):
    same_doc = seg_query[:, None] == seg_key[None, :]
    causal = pos_key[None, :] <= pos_query[:, None]
    self_only = (seg_query[:, None] >= 0) | (pos_key[None, :] == pos_query[:, None])
    return same_doc & causal & self_only

def adamw_update(weight, first_moment, second, gradient, step_rate, decay_rate):
    first_moment = beta_one * first_moment + (1.0 - beta_one) * gradient
    second = beta_two * second + (1.0 - beta_two) * gradient * gradient
    first_hat = first_moment / (1.0 - beta_one ** STEP)
    second_hat = second / (1.0 - beta_two ** STEP)
    weight = weight - step_rate * (first_hat / (jnp.sqrt(second_hat) + adam_eps) + decay_rate * weight)
    return (weight, first_moment, second)

def block_forward(hidden, seg_ids, attn_w, mlp_w, vec_w):
    pieces = [vec_w[number * D:(number + 1) * D] for number in range(8)]
    gain_one, shift_one, bias_query, bias_value, bias_out, gain_two, shift_two, bias_down = pieces
    bias_up = vec_w[8 * D:]
    row_count = hidden.shape[0]
    head_shape = (row_count, HEADS, HEAD_DIM)
    first_in = low(normalize(hidden, gain_one, shift_one))
    projected = jnp.dot(first_in, attn_w[:, :3 * D], precision=highest)
    query_heads = low_back(low(projected[:, :D] + bias_query)).reshape(head_shape)
    key_heads = low_back(low(projected[:, D:2 * D])).reshape(head_shape)
    value_heads = low_back(low(projected[:, 2 * D:] + bias_value)).reshape(head_shape)
    scores = low_back(jnp.einsum('qhd,khd->hqk', query_heads, key_heads, precision=highest) * HEAD_DIM ** (-0.5))
    positions = jnp.arange(row_count)
    allowed = permitted(seg_ids, seg_ids, positions, positions)
    masked = jnp.where(allowed[None], scores, neg_large)
    row_max = lax.optimization_barrier(jnp.max(masked, axis=-1, keepdims=True))
    log_total = row_max + jnp.log(lax.optimization_barrier(jnp.sum(jnp.exp(masked - row_max), axis=-1, keepdims=True)))
    attn_probs = low(jnp.exp(masked - log_total))
    mixed_rows = jnp.einsum('hqk,khd->qhd', attn_probs, value_heads, precision=highest).reshape(row_count, D)
    mixed_rows = low_back(low(mixed_rows))
    residual = hidden + low_back(jnp.dot(mixed_rows, attn_w[:, 3 * D:], precision=highest) + bias_out)
    second_in = low(normalize(residual, gain_two, shift_two))
    pre_act = low_back(jnp.dot(second_in, mlp_w[:, :FF], precision=highest) + bias_up)
    act_low = low(gelu_tanh(pre_act))
    down_out = lax.dot_general(act_low, mlp_w[:, FF:], (((1,), (1,)), ((), ())), precision=highest)
    return residual + down_out + bias_down

def reference(tokens, segment, cotangent, w_attn, m_attn, v_attn, w_mlp, m_mlp, v_mlp, vectors, m_vec, v_vec):
    block_count = TOKENS // TOK_DEV

    def forward(hidden, attn_w, mlp_w, vec_w):
        attn_low = low(attn_w)
        mlp_low = low(mlp_w)
        vec_low = low(vec_w)

        def one_block(block_pair):
            return block_forward(block_pair[0], block_pair[1], attn_low, mlp_low, vec_low)
        stacked = (hidden.reshape(block_count, TOK_DEV, D), segment.reshape(block_count, TOK_DEV))
        outputs = lax.map(jax.checkpoint(one_block), stacked)
        return outputs.reshape(TOKENS, D)
    hidden = tokens.astype(jnp.float32)
    result, pullback = jax.vjp(forward, hidden, w_attn, w_mlp, vectors)
    grad_out = jnp.where((segment >= 0)[:, None], cotangent.astype(jnp.float32), 0.0)
    input_grad, grad_attn, grad_mlp, grad_vec = pullback(grad_out)
    new_attn, first_attn, second_attn = adamw_update(w_attn, m_attn, v_attn, grad_attn, matrix_rate, matrix_decay)
    new_mlp, first_mlp, second_mlp = adamw_update(w_mlp, m_mlp, v_mlp, grad_mlp, matrix_rate, matrix_decay)
    new_vec, first_vec, second_vec = adamw_update(vectors, m_vec, v_vec, grad_vec, vector_rate, 0.0)
    return (result.astype(jnp.bfloat16), input_grad, new_attn, first_attn, second_attn, new_mlp, first_mlp, second_mlp, new_vec, first_vec, second_vec)
```

```python
import functools
import math

import jax
import jax.numpy as jnp
from jax import lax
from jax.experimental import pallas as pl
from jax.experimental.pallas import tpu as pltpu
from jax.sharding import PartitionSpec as P

D = 384
HEADS = 6
HEAD_DIM = 64
FF = 1536
TOK = 512
QBLK = 256
STEP = 10
VEC_ROWS = 16

norm_eps = 1e-05
beta_one = 0.9
beta_two = 0.95
adam_eps = 1e-08
matrix_rate = 0.15
vector_rate = 0.6
matrix_decay = 0.1
neg_large = -1e30
gelu_c = math.sqrt(2.0 / math.pi)

f32 = jnp.float32
bf16 = jnp.bfloat16
VMEM_BYTES = 48 * 1024 * 1024

vmem = pl.BlockSpec(memory_space=pltpu.VMEM)
smem = pl.BlockSpec(memory_space=pltpu.SMEM)


def dot(left, right, dims):
    return lax.dot_general(left, right, ((dims[:1], dims[1:]), ((), ())), preferred_element_type=f32)


def mm(left, right):
    return dot(left, right, (1, 0))


def mm_nt(left, right):
    return dot(left, right, (1, 1))


def mm_tn(left, right):
    return dot(left, right, (0, 0))


def ln_parts(values):
    mean = jnp.mean(values, axis=-1, keepdims=True)
    centred = values - mean
    var = jnp.mean(centred * centred, axis=-1, keepdims=True)
    rstd = lax.rsqrt(var + norm_eps)
    return centred * rstd, rstd


def ln_back(grad, gain, normed, rstd):
    e = grad * gain
    mean_e = jnp.mean(e, axis=-1, keepdims=True)
    mean_en = jnp.mean(e * normed, axis=-1, keepdims=True)
    return (e - mean_e - normed * mean_en) * rstd


def call(kernel, outs, ins, args, scratch=(), flops=0, name=None):
    moved = sum(math.prod(a.shape) * a.dtype.itemsize for a in args)
    moved += sum(math.prod(o.shape) * o.dtype.itemsize for o in outs)
    return pl.pallas_call(
        kernel,
        out_shape=list(outs),
        in_specs=list(ins),
        out_specs=[vmem] * len(outs),
        scratch_shapes=list(scratch),
        compiler_params=pltpu.CompilerParams(vmem_limit_bytes=VMEM_BYTES),
        cost_estimate=pl.CostEstimate(flops=flops, bytes_accessed=moved, transcendentals=0),
        name=name,
    )(*args)


def shaped(shape, dtype):
    return jax.ShapeDtypeStruct(shape, dtype)


class Plan:
    def __init__(self, mesh):
        self.n_dp = mesh.shape["dp"]
        self.n_opt = mesh.shape["opt"]
        self.n_z = self.n_dp // 4
        self.own = D // self.n_opt
        self.chunk = self.own // self.n_z
        self.unit = math.gcd(self.chunk, 16)
        self.per = self.chunk // self.unit
        self.vec_units = VEC_ROWS // self.unit


def assemble(plan, idx_ref, own_ref, direct_refs, cross_refs, full_ref):
    core, op = idx_ref[0], idx_ref[3]
    width = full_ref.shape[3]
    full_ref[op, 0] = own_ref[:, :width].astype(bf16)
    full_ref[op, 1] = own_ref[:, width:].astype(bf16)
    for m in range(1, plan.n_opt):
        full_ref[op ^ m, core] = direct_refs[m - 1][: plan.own, :]
        full_ref[op ^ m, 1 - core] = cross_refs[m - 1][: plan.own, :]


def store_chunks(plan, ref, base_of, value, mats, mat, idx_ref):
    zi, op = idx_ref[2], idx_ref[3]
    for i in range(plan.n_opt * plan.n_z):
        rel = ((i // plan.n_z) ^ op) * plan.n_z + ((i % plan.n_z) ^ zi)
        for t in range(plan.per):
            row = i * plan.chunk + t * plan.unit
            at = base_of + (rel * mats + mat) * plan.per + t
            ref[at] = value[row : row + plan.unit].astype(ref.dtype)


def attn_forward(plan, *refs):
    n = plan.n_opt - 1
    idx_ref, tok_ref, segc_ref, segr_ref, vec_ref, own_ref = refs[:6]
    direct_refs, cross_refs = refs[6 : 6 + n], refs[6 + n : 6 + 2 * n]
    full_ref, qkv_ref, mixed_ref, lse_ref, resid_ref, bias_ref = refs[6 + 2 * n :]
    assemble(plan, idx_ref, own_ref, direct_refs, cross_refs, full_ref)
    hidden = tok_ref[...].astype(f32)
    normed, _ = ln_parts(hidden)
    first_in = (normed * vec_ref[0:1, :] + vec_ref[1:2, :]).astype(bf16)
    for number, row in ((0, 2), (1, None), (2, 3)):
        lane = (number % 2) * D
        weight = full_ref[:, number // 2, :, lane : lane + D].reshape(D, D)
        part = mm(first_in, weight)
        if row is not None:
            part = part + vec_ref[row : row + 1, :]
        qkv_ref[number] = part.astype(bf16).T
    fill_bias(segc_ref, segr_ref, bias_ref)

    def one_head(head, carry):
        rows = pl.ds(pl.multiple_of(head * HEAD_DIM, HEAD_DIM), HEAD_DIM)
        for blk in range(TOK // QBLK):
            cols = slice(blk * QBLK, (blk + 1) * QBLK)
            keys = (blk + 1) * QBLK
            query = qkv_ref[0, rows, cols] * bf16(HEAD_DIM**-0.5)
            scores = mm_tn(qkv_ref[1, rows, :keys], query) + bias_ref[:keys, cols]
            top = jnp.max(scores, axis=0, keepdims=True)
            e = jnp.exp(scores - top)
            total = jnp.sum(e, axis=0, keepdims=True)
            probs = (e * (1.0 / total)).astype(bf16)
            mixed_ref[rows, cols] = mm(qkv_ref[2, rows, :keys], probs).astype(bf16)
            lse_ref[pl.ds(head, 1), :, cols] = (top + jnp.log(total)).reshape(1, 1, QBLK)
        return carry

    lax.fori_loop(0, HEADS, one_head, 0, unroll=True)
    out_weight = full_ref[:, 1, :, D:].reshape(D, D)
    resid_ref[...] = hidden + (mm_tn(mixed_ref[...], out_weight) + vec_ref[4:5, :])


def fill_bias(segc_ref, segr_ref, bias_ref):
    key = lax.broadcasted_iota(jnp.int32, (TOK, TOK), 0)
    query = lax.broadcasted_iota(jnp.int32, (TOK, TOK), 1)
    seg_query = segr_ref[...]
    allowed = (segc_ref[...] == seg_query) & (key <= query) & ((seg_query >= 0) | (key == query))
    bias_ref[...] = jnp.where(allowed, 0.0, neg_large)


def mlp_step(plan, *refs):
    n = plan.n_opt - 1
    idx_ref, resid_ref, cot_ref, segc_ref, vec_ref, bup_ref, own_ref = refs[:7]
    direct_refs, cross_refs = refs[7 : 7 + n], refs[7 + n : 7 + 2 * n]
    (keep_ref, send_ref, act_ref, dres_ref, gvec_ref, gbup_ref, full_ref, out_acc, db_acc) = refs[7 + 2 * n :]
    assemble(plan, idx_ref, own_ref, direct_refs, cross_refs, full_ref)
    core, ybit = idx_ref[0], idx_ref[1]
    resid = resid_ref[...]
    normed, rstd = ln_parts(resid)
    second_in = (normed * vec_ref[5:6, :] + vec_ref[6:7, :]).astype(bf16)
    second_t = second_in.T
    dy = jnp.where(segc_ref[...] >= 0, cot_ref[...].astype(f32), 0.0)
    dy_low = dy.astype(bf16)
    dy_t = dy_low.T
    out_acc[...] = jnp.zeros_like(out_acc)
    db_acc[...] = jnp.zeros_like(db_acc)
    wide = FF // 2
    units = plan.n_opt * plan.n_z * 2 * plan.per

    def one_block(blk, carry):
        cols = pl.ds(pl.multiple_of(blk * wide, wide), wide)
        up = full_ref[:, 0, :, cols].reshape(D, wide)
        down = full_ref[:, 1, :, cols].reshape(D, wide)
        pre = mm(second_in, up) + bup_ref[blk]
        sq = pre * pre
        th = jnp.tanh(gelu_c * pre * (1.0 + 0.044715 * sq))
        half = 0.5 * (1.0 + th)
        act = (pre * half).astype(bf16)
        slope = half + (0.5 * gelu_c) * pre * (1.0 - th * th) * (1.0 + (3 * 0.044715) * sq)
        out_acc[...] += mm_nt(act, down)
        dpre = (mm(dy_low, down) * slope).astype(bf16)
        gbup_ref[blk] = jnp.sum(dpre.astype(f32), axis=0, keepdims=True)
        db_acc[...] += mm_nt(dpre, up)
        base = (blk ^ ybit) * units
        for mat, (left, right) in enumerate(((second_t, dpre), (dy_t, act))):
            grad = mm(left, right)
            first, last = grad[:, :D], grad[:, D:]
            store_chunks(plan, keep_ref, base, jnp.where(core == 0, first, last), 2, mat, idx_ref)
            store_chunks(plan, send_ref, base, jnp.where(core == 0, last, first), 2, mat, idx_ref)
        return carry

    lax.fori_loop(0, 2, one_block, 0, unroll=True)
    act_ref[...] = (resid + out_acc[...] + vec_ref[7:8, :]).astype(bf16)
    db = db_acc[...]
    dres_ref[...] = dy + ln_back(db, vec_ref[5:6, :], normed, rstd)
    gvec_ref[0:1, :] = jnp.sum(db * normed, axis=0, keepdims=True)
    gvec_ref[1:2, :] = jnp.sum(db, axis=0, keepdims=True)
    gvec_ref[2:3, :] = jnp.sum(dy, axis=0, keepdims=True)
    gvec_ref[3:8, :] = jnp.zeros((5, D), f32)


def back_heads(first, last, qkv_ref, bias_ref, lse_ref, dmix_ref, dqkv_ref, dkv_acc):
    scale = HEAD_DIM**-0.5
    for head in range(first, last):
        rows = slice(head * HEAD_DIM, (head + 1) * HEAD_DIM)
        out_rows = slice((head - first) * HEAD_DIM, (head - first + 1) * HEAD_DIM)
        for blk in range(TOK // QBLK):
            cols = slice(blk * QBLK, (blk + 1) * QBLK)
            keys = (blk + 1) * QBLK
            query = qkv_ref[0, rows, cols]
            key = qkv_ref[1, rows, :keys]
            value = qkv_ref[2, rows, :keys]
            dmix = dmix_ref[rows, cols]
            scores = mm_tn(key, query * bf16(scale)) + bias_ref[:keys, cols]
            probs = jnp.exp(scores - lse_ref[head][:, cols])
            dprobs = mm_tn(value, dmix)
            row_dot = jnp.sum(probs * dprobs, axis=0, keepdims=True)
            dscores = (probs * (dprobs - row_dot)).astype(bf16)
            dqkv_ref[0, out_rows, cols] = (mm(key, dscores) * scale).astype(bf16)
            dkey = mm_nt(query, dscores)
            dvalue = mm_nt(dmix, probs.astype(bf16))
            if blk == 0:
                dkv_acc[0, :, :QBLK] = dkey
                dkv_acc[1, :, :QBLK] = dvalue
            else:
                dkv_acc[0, :, :QBLK] += dkey[:, :QBLK]
                dkv_acc[1, :, :QBLK] += dvalue[:, :QBLK]
                dkv_acc[0, :, QBLK:] = dkey[:, QBLK:]
                dkv_acc[1, :, QBLK:] = dvalue[:, QBLK:]
        dqkv_ref[1, out_rows, :] = (dkv_acc[0] * scale).astype(bf16)
        dqkv_ref[2, out_rows, :] = dkv_acc[1].astype(bf16)


def attn_back_first(last, segc_ref, segr_ref, dres_ref, full_ref, mixed_ref, qkv_ref, lse_ref,
                    dmix_ref, gout_ref, gbo_ref, dqkv_ref, bias_ref, dkv_acc):
    dz = dres_ref[...].astype(bf16)
    gbo_ref[...] = jnp.broadcast_to(jnp.sum(dz.astype(f32), axis=0, keepdims=True), (8, D))
    out_weight = full_ref[:, 1, :, D:].reshape(D, D)
    dmix_ref[...] = mm_nt(out_weight, dz).astype(bf16)
    gout_ref[...] = mm(mixed_ref[...], dz)
    fill_bias(segc_ref, segr_ref, bias_ref)
    back_heads(0, last, qkv_ref, bias_ref, lse_ref, dmix_ref, dqkv_ref, dkv_acc)


def attn_back_next(first, last, segc_ref, segr_ref, dmix_ref, qkv_ref, lse_ref, dqkv_ref, bias_ref, dkv_acc):
    fill_bias(segc_ref, segr_ref, bias_ref)
    back_heads(first, last, qkv_ref, bias_ref, lse_ref, dmix_ref, dqkv_ref, dkv_acc)


def attn_back_last(plan, count, *refs):
    idx_ref, tok_ref, dres_ref, full_ref, vec_ref, gout_ref, gbo_ref, gvec_ref, gbup_ref = refs[:9]
    parts = refs[9 : 9 + count]
    keep_ref, send_ref, igrad_ref = refs[9 + count :]
    core, ybit = idx_ref[0], idx_ref[1]
    hidden = tok_ref[...].astype(f32)
    normed, rstd = ln_parts(hidden)
    first_in = (normed * vec_ref[0:1, :] + vec_ref[1:2, :]).astype(bf16)
    first_t = first_in.T
    dqkv = [jnp.concatenate([part[number] for part in parts], axis=0) for number in range(3)]
    grads = [mm_nt(first_t, dpart) for dpart in dqkv] + [gout_ref[...]]
    units = plan.n_opt * plan.n_z * plan.per
    for pair in range(2):
        base = (pair ^ ybit) * units
        first, last = grads[2 * pair], grads[2 * pair + 1]
        store_chunks(plan, keep_ref, base, jnp.where(core == 0, first, last), 1, 0, idx_ref)
        store_chunks(plan, send_ref, base, jnp.where(core == 0, last, first), 1, 0, idx_ref)
    da_t = jnp.zeros((D, TOK), f32)
    for number in range(3):
        lane = (number % 2) * D
        weight = full_ref[:, number // 2, :, lane : lane + D].reshape(D, D)
        da_t = da_t + mm(weight, dqkv[number])
    da = da_t.T
    igrad_ref[...] = dres_ref[...] + ln_back(da, vec_ref[0:1, :], normed, rstd)
    ones = jnp.ones((8, TOK), bf16)
    rows = [
        jnp.sum(da * normed, axis=0, keepdims=True),
        jnp.sum(da, axis=0, keepdims=True),
        mm_nt(ones, dqkv[0])[0:1, :],
        mm_nt(ones, dqkv[2])[0:1, :],
        gbo_ref[0:1, :],
        gvec_ref[0:3, :],
    ]
    for blk in range(2):
        rows += [gbup_ref[blk][:, :D], gbup_ref[blk][:, D:]]
    rows.append(jnp.zeros((VEC_ROWS - 12, D), f32))
    total = jnp.concatenate(rows, axis=0)
    for t in range(plan.vec_units):
        piece = total[t * plan.unit : (t + 1) * plan.unit]
        keep_ref[2 * units + t] = piece
        send_ref[2 * units + t] = piece.astype(bf16)


def add_pieces(count, size, tail, keep_dtype, *refs):
    keep_ref, others, outs = refs[0], refs[1 : -count], refs[-count:]
    for number in range(count):
        part = pl.ds(number * size, size)
        total = keep_ref[part].astype(f32)
        for other in others:
            total = total + other[part].astype(f32)
        outs[number][:size] = total.astype(outs[number].dtype)
    if tail:
        part = pl.ds(count * size, tail)
        total = keep_ref[part].astype(f32)
        for other in others:
            total = total + other[part].astype(f32)
        for number in range(count):
            outs[number][size:] = total.astype(outs[number].dtype)


def add_last(size, tail, keep_ref, *refs):
    others, outs = refs[: -(2 if tail else 1)], refs[-(2 if tail else 1) :]
    total = keep_ref[...]
    for other in others:
        total = total + other[...].astype(f32)
    outs[0][...] = total[:size].astype(bf16)
    if tail:
        outs[1][...] = total[size:]


def swap_core(n_dp, value):
    return lax.ppermute(value, "dp", [(i, i ^ 1) for i in range(n_dp)])


def reduce_scatter(plan, keep, send, mats, tail, tag):
    n_dp, n_opt, n_z = plan.n_dp, plan.n_opt, plan.n_z
    lead = plan.unit
    got = swap_core(n_dp, send)
    count = 2 * n_opt
    size = n_z * mats * plan.per
    outs = [shaped((size + tail, lead, D), f32 if k == 0 else bf16) for k in range(count)]
    parts = call(
        functools.partial(add_pieces, count, size, tail, f32), outs, [vmem] * 2, [keep, got], name="add_core_" + tag
    )
    got = []
    for number in range(1, count):
        mask_y, mask_o = number // n_opt, number % n_opt
        perm = [
            ((d * n_opt + o), ((d ^ (2 * mask_y)) * n_opt + (o ^ mask_o))) for d in range(n_dp) for o in range(n_opt)
        ]
        got.append(lax.ppermute(parts[number], ("dp", "opt"), perm))
    size = mats * plan.per
    outs = [shaped((size + tail, lead, D), f32 if k == 0 else bf16) for k in range(n_z)]
    parts = call(
        functools.partial(add_pieces, n_z, size, tail, f32),
        outs,
        [vmem] * count,
        [parts[0], *got],
        name="add_plane_" + tag,
    )
    got = [lax.ppermute(parts[m], "dp", [(i, i ^ (4 * m)) for i in range(n_dp)]) for m in range(1, n_z)]
    outs = [shaped((size, lead, D), bf16)]
    if tail:
        outs.append(shaped((tail, lead, D), f32))
    return call(
        functools.partial(add_last, size, tail), outs, [vmem] * n_z, [parts[0], *got], name="add_column_" + tag
    )


def gather(plan, shard):
    n_dp = plan.n_dp
    got = [lax.ppermute(shard, "dp", [(i, i ^ (4 * m)) for i in range(n_dp)]) for m in range(1, plan.n_z)]
    column = jnp.concatenate([shard, *got], axis=0)
    far = lax.ppermute(column, "dp", [(i, i ^ 2) for i in range(n_dp)])
    return column, swap_core(n_dp, column), far, swap_core(n_dp, far)


def adamw(weight, first, second, grad, rate, decay):
    first = beta_one * first + (1.0 - beta_one) * grad
    second = beta_two * second + (1.0 - beta_two) * grad * grad
    first_hat = first * (1.0 / (1.0 - beta_one**STEP))
    second_hat = second * (1.0 / (1.0 - beta_two**STEP))
    weight = weight - rate * (first_hat / (jnp.sqrt(second_hat) + adam_eps) + decay * weight)
    return weight, first, second


def adam_kernel(plan, mats, idx_ref, g0, g1, g2, g3, w_ref, m_ref, v_ref, nw_ref, nm_ref, nv_ref):
    mat = pl.program_id(0) // 4
    rel = (pl.program_id(0) % 4) ^ (idx_ref[0] + 2 * idx_ref[1])
    zi = idx_ref[2]
    for z in range(plan.n_z):
        for t in range(plan.per):
            at = ((z ^ zi) * mats + mat) * plan.per + t
            near = jnp.where(rel == 0, g0[at], g1[at])
            far = jnp.where(rel == 2, g2[at], g3[at])
            grad = jnp.where(rel < 2, near, far).astype(f32)
            rows = slice(z * plan.chunk + t * plan.unit, z * plan.chunk + (t + 1) * plan.unit)
            out = adamw(w_ref[rows], m_ref[rows], v_ref[rows], grad, matrix_rate, matrix_decay)
            nw_ref[rows], nm_ref[rows], nv_ref[rows] = out


def adam_matrix(plan, idx, grads, weight, first, second, mats):
    block = pl.BlockSpec((plan.own, D), lambda i: (0, i))
    whole = pl.BlockSpec(grads[0].shape, lambda i: (0, 0, 0))
    shape = shaped(weight.shape, f32)
    return pl.pallas_call(
        functools.partial(adam_kernel, plan, mats),
        grid=(4 * mats,),
        out_shape=[shape] * 3,
        in_specs=[smem] + [whole] * 4 + [block] * 3,
        out_specs=[block] * 3,
        compiler_params=pltpu.CompilerParams(vmem_limit_bytes=VMEM_BYTES),
        cost_estimate=pl.CostEstimate(
            flops=16 * weight.size, bytes_accessed=24 * weight.size, transcendentals=weight.size
        ),
        name="adam_" + str(mats),
    )(idx, *grads, weight, first, second)


def body(plan, tokens, segment, cotangent, w_attn, m_attn, v_attn, w_mlp, m_mlp, v_mlp, vectors, m_vec, v_vec):
    n_dp, n_opt = plan.n_dp, plan.n_opt
    dp, op = lax.axis_index("dp"), lax.axis_index("opt")
    core = dp & 1
    idx = jnp.stack([core, (dp >> 1) & 1, dp >> 2, op]).astype(jnp.int32)
    segc, segr = segment.reshape(TOK, 1), segment.reshape(1, TOK)

    def spread(send):
        direct = [
            lax.ppermute(send, "opt", [(o, o ^ m) for o in range(n_opt)]) for m in range(1, n_opt)
        ]
        return direct, [swap_core(n_dp, piece) for piece in direct]

    width = 2 * D
    length = vectors.shape[0]
    vec_rows = -(-length // width)
    vec_pad = jnp.pad(vectors.astype(bf16), (0, 16 * width - length)).reshape(16, width)
    attn_half = lax.dynamic_slice(w_attn, (0, core * width), (plan.own, width)).astype(bf16)
    attn_direct, attn_cross = spread(jnp.concatenate([attn_half, vec_pad], axis=0))
    mlp_half = lax.dynamic_slice(w_mlp, (0, core * FF), (plan.own, FF)).astype(bf16)
    mlp_direct, mlp_cross = spread(mlp_half)
    vec_parts = [vectors.astype(bf16)] + [
        piece[plan.own : plan.own + vec_rows].reshape(-1)[:length] for piece in attn_direct
    ]
    if n_opt == 2:
        low = jnp.where(op == 0, vec_parts[0], vec_parts[1])
        high = jnp.where(op == 0, vec_parts[1], vec_parts[0])
        vec = jnp.concatenate([low, high])
    else:
        vec = jnp.stack(vec_parts)[jnp.arange(n_opt) ^ op].reshape(-1)
    vec = vec.astype(f32)
    vec8 = vec[: 8 * D].reshape(8, D)
    bup = vec[8 * D :].reshape(2, 1, FF // 2)

    full, qkv, mixed, lse, resid = call(
        functools.partial(attn_forward, plan),
        [
            shaped((n_opt, 2, plan.own, width), bf16),
            shaped((3, D, TOK), bf16),
            shaped((D, TOK), bf16),
            shaped((HEADS, 1, TOK), f32),
            shaped((TOK, D), f32),
        ],
        [smem] + [vmem] * (5 + 2 * (n_opt - 1)),
        [idx, tokens, segc, segr, vec8, w_attn, *attn_direct, *attn_cross],
        [pltpu.VMEM((TOK, TOK), f32)],
        flops=2 * TOK * D * 4 * D + 8 * TOK * TOK * D,
        name="attn_forward",
    )
    units = 2 * n_opt * plan.n_z * plan.per
    mlp_keep, mlp_send, activations, dres, gvec, gbup = call(
        functools.partial(mlp_step, plan),
        [
            shaped((2 * units, plan.unit, D), f32),
            shaped((2 * units, plan.unit, D), bf16),
            shaped((TOK, D), bf16),
            shaped((TOK, D), f32),
            shaped((8, D), f32),
            shaped((2, 1, FF // 2), f32),
        ],
        [smem] + [vmem] * (6 + 2 * (n_opt - 1)),
        [idx, resid, cotangent, segc, vec8, bup, w_mlp, *mlp_direct, *mlp_cross],
        [
            pltpu.VMEM((n_opt, 2, plan.own, FF), bf16),
            pltpu.VMEM((TOK, D), f32),
            pltpu.VMEM((TOK, D), f32),
        ],
        flops=12 * TOK * D * FF,
        name="mlp_step",
    )
    (mlp_shard,) = reduce_scatter(plan, mlp_keep, mlp_send, 2, 0, "mlp")
    mlp_grads = gather(plan, mlp_shard)

    head_flops = 14 * TOK * TOK * HEAD_DIM
    head_scratch = [pltpu.VMEM((TOK, TOK), f32), pltpu.VMEM((2, HEAD_DIM, TOK), f32)]
    cuts = (0, 2, 4, 6)
    dmix, gout, gbo, part = call(
        functools.partial(attn_back_first, cuts[1]),
        [
            shaped((D, TOK), bf16),
            shaped((D, D), f32),
            shaped((8, D), f32),
            shaped((3, cuts[1] * HEAD_DIM, TOK), bf16),
        ],
        [vmem] * 7,
        [segc, segr, dres, full, mixed, qkv, lse],
        head_scratch,
        flops=4 * TOK * D * D + cuts[1] * head_flops,
        name="attn_back_first",
    )
    parts = [part]
    for first, last in zip(cuts[1:-1], cuts[2:]):
        (part,) = call(
            functools.partial(attn_back_next, first, last),
            [shaped((3, (last - first) * HEAD_DIM, TOK), bf16)],
            [vmem] * 5,
            [segc, segr, dmix, qkv, lse],
            head_scratch,
            flops=(last - first) * head_flops,
            name="attn_back_next",
        )
        parts.append(part)
    attn_keep, attn_send, input_grad = call(
        functools.partial(attn_back_last, plan, len(parts)),
        [
            shaped((units + plan.vec_units, plan.unit, D), f32),
            shaped((units + plan.vec_units, plan.unit, D), bf16),
            shaped((TOK, D), f32),
        ],
        [smem] + [vmem] * (8 + len(parts)),
        [idx, tokens, dres, full, vec8, gout, gbo, gvec, gbup, *parts],
        flops=12 * TOK * D * D,
        name="attn_back_last",
    )
    attn_shard, vec_grad = reduce_scatter(plan, attn_keep, attn_send, 1, plan.vec_units, "attn")
    attn_grads = gather(plan, attn_shard)
    new_mlp, first_mlp, second_mlp = adam_matrix(plan, idx, mlp_grads, w_mlp, m_mlp, v_mlp, 2)
    new_attn, first_attn, second_attn = adam_matrix(plan, idx, attn_grads, w_attn, m_attn, v_attn, 1)
    own_vec = lax.dynamic_slice(vec_grad.reshape(-1), (op * length,), (length,))
    new_vec, first_vec, second_vec = adamw(vectors, m_vec, v_vec, own_vec, vector_rate, 0.0)
    return (
        activations,
        input_grad,
        new_attn,
        first_attn,
        second_attn,
        new_mlp,
        first_mlp,
        second_mlp,
        new_vec,
        first_vec,
        second_vec,
    )


def solution(mesh):
    rows, both = P("opt", None), P(("dp", "opt"), None)
    in_specs = (both, P(("dp", "opt")), both) + (rows,) * 6 + (P("opt"),) * 3
    out_specs = (both, both) + (rows,) * 6 + (P("opt"),) * 3
    return jax.shard_map(
        functools.partial(body, Plan(mesh)), mesh=mesh, in_specs=in_specs, out_specs=out_specs, check_vma=False
    )
```

```python
import functools
import math

import jax
import jax.numpy as jnp
from jax import lax
from jax.experimental import pallas as pl
from jax.experimental.pallas import tpu as pltpu
from jax.sharding import PartitionSpec as P

D = 384
HEADS = 6
HEAD_DIM = 64
FF = 1536
TOK = 512
QBLK = 256
STEP = 10
VEC_ROWS = 16

norm_eps = 1e-05
beta_one = 0.9
beta_two = 0.95
adam_eps = 1e-08
matrix_rate = 0.15
vector_rate = 0.6
matrix_decay = 0.1
neg_large = -1e30
gelu_c = math.sqrt(2.0 / math.pi)

f32 = jnp.float32
bf16 = jnp.bfloat16
MIB = 1024 * 1024
HOLD = False
ROWS = 96
MLP_CUT = (1536,)

vmem = pl.BlockSpec(memory_space=pltpu.VMEM)


def dot(left, right, dims):
    return lax.dot_general(left, right, ((dims[:1], dims[1:]), ((), ())), preferred_element_type=f32)


def mm(left, right):
    return dot(left, right, (1, 0))


def mm_nt(left, right):
    return dot(left, right, (1, 1))


def mm_tn(left, right):
    return dot(left, right, (0, 0))


def ln_parts(values):
    mean = jnp.mean(values, axis=-1, keepdims=True)
    centred = values - mean
    var = jnp.mean(centred * centred, axis=-1, keepdims=True)
    rstd = lax.rsqrt(var + norm_eps)
    return centred * rstd, rstd


def ln_back(grad, gain, normed, rstd):
    e = grad * gain
    mean_e = jnp.mean(e, axis=-1, keepdims=True)
    mean_en = jnp.mean(e * normed, axis=-1, keepdims=True)
    return (e - mean_e - normed * mean_en) * rstd


def after(value, *others):
    return lax.optimization_barrier((value, *others))[0]


def call(kernel, outs, ins, args, scratch=(), flops=0, name=None, room=12, light=False):
    moved = sum(math.prod(a.shape) * a.dtype.itemsize for a in args)
    moved += sum(math.prod(o.shape) * o.dtype.itemsize for o in outs)
    return pl.pallas_call(
        kernel,
        out_shape=list(outs),
        in_specs=list(ins),
        out_specs=[vmem] * len(outs),
        scratch_shapes=list(scratch),
        compiler_params=pltpu.CompilerParams(vmem_limit_bytes=room * MIB),
        cost_estimate=pl.CostEstimate(
            flops=0 if light else flops, bytes_accessed=0 if light else moved, transcendentals=0
        ),
        name=name,
    )(*args)


def shaped(shape, dtype):
    return jax.ShapeDtypeStruct(shape, dtype)


class Plan:
    def __init__(self, mesh):
        self.n_dp = mesh.shape["dp"]
        self.n_opt = mesh.shape["opt"]
        self.n_z = self.n_dp // 4
        self.own = D // self.n_opt
        self.attn = Stream(self, "attn", 1, 1, VEC_ROWS)
        self.mlp = Stream(self, "mlp", 2, 2, 0)


class Stream:
    def __init__(self, plan, name, mats, split, tail):
        self.name, self.mats, self.split = name, mats, split
        self.chunk = plan.own // split
        self.unit = math.gcd(self.chunk, 16)
        self.per = self.chunk // self.unit
        self.tail = tail // self.unit
        self.shard = mats * self.per
        self.places = 2 * plan.n_opt
        self.piece = split * self.shard
        self.total = self.places * self.piece


def position():
    dp, op = lax.axis_index("dp"), lax.axis_index("opt")
    return dp & 1, (dp >> 1) & 1, dp >> 2, op


def assemble(plan, own_ref, direct, cross, full_ref):
    core, _, _, op = position()
    width = full_ref.shape[3]
    full_ref[op, 0] = own_ref[:, :width]
    full_ref[op, 1] = own_ref[:, width:]
    for half, messages in ((core, direct), (1 - core, cross)):
        lane = 0
        for pieces in messages:
            cols = slice(lane, lane + pieces[0].shape[1])
            lane += pieces[0].shape[1]
            for m in range(1, plan.n_opt):
                full_ref[op ^ m, half, :, cols] = pieces[m - 1][: plan.own, :]


def store_chunks(plan, stream, ref, base, value, mat):
    _, _, zi, op = position()
    for i in range(plan.n_opt * stream.split):
        rel = ((i // stream.split) ^ op) * stream.split + ((i % stream.split) ^ (zi & (stream.split - 1)))
        for t in range(stream.per):
            row = i * stream.chunk + t * stream.unit
            at = base + (rel * stream.mats + mat) * stream.per + t
            ref[at] = value[row : row + stream.unit].astype(ref.dtype)


def split_sends(stream, whole_ref, refs):
    for number, ref in enumerate(refs):
        ref[...] = whole_ref[number * stream.piece : (number + 1) * stream.piece]


def column_of(row):
    return jnp.broadcast_to(row.astype(f32), (8, TOK)).T[:, :1]


def fill_bias(seg_ref, bias_ref):
    key = lax.broadcasted_iota(jnp.int32, (TOK, TOK), 0)
    query = lax.broadcasted_iota(jnp.int32, (TOK, TOK), 1)
    seg_query = seg_ref[...].astype(f32)
    allowed = (column_of(seg_ref[...]) == seg_query) & (key <= query) & ((seg_query >= 0) | (key == query))
    bias_ref[...] = jnp.where(allowed, 0.0, neg_large)


def spread_vec(plan, length, own_ref, direct, piece_ref, vec_ref, bup_ref):
    _, _, _, op = position()
    size = piece_ref.shape[2]
    count, width = length // size, own_ref.shape[1]
    for m in range(plan.n_opt):
        ref = own_ref if m == 0 else direct[m - 1]
        rows = ref[plan.own : plan.own + 16, :].astype(f32)
        for k in range(count):
            row, lane = (k * size) // width, (k * size) % width
            piece_ref[(op ^ m) * count + k] = rows[row : row + 1, lane : lane + size]
    per = D // size

    def row_of(number):
        return jnp.concatenate([piece_ref[number * per + k] for k in range(per)], axis=1)

    for number in range(8):
        vec_ref[number : number + 1, :] = row_of(number)
    for blk in range(2):
        bup_ref[blk] = jnp.concatenate([row_of(8 + 2 * blk), row_of(9 + 2 * blk)], axis=1)


def cast_weights(plan, attn_ref, mlp_ref, attn_low, mlp_low, *halves):
    core = position()[0]
    attn_low[...] = attn_ref[...].astype(bf16)
    mlp_low[...] = mlp_ref[...].astype(bf16)
    lane = 0
    for ref in halves:
        start = pl.multiple_of(core * FF + lane, 128)
        ref[...] = mlp_low[:, pl.ds(start, ref.shape[1])]
        lane += ref.shape[1]


def attn_forward(plan, length, *refs):
    n = plan.n_opt - 1
    tok_ref, seg_ref, own_ref, sent_ref = refs[:4]
    direct, cross = refs[4 : 4 + n], refs[4 + n : 4 + 2 * n]
    full_ref, qkv_ref, mixed_ref, lse_ref, resid_ref, vec_ref, bup_ref, bias_ref, piece_ref = refs[4 + 2 * n :]
    assemble(plan, own_ref, [direct], [cross], full_ref)
    spread_vec(plan, length, sent_ref, direct, piece_ref, vec_ref, bup_ref)
    hidden = tok_ref[...].astype(f32)
    normed, _ = ln_parts(hidden)
    first_in = (normed * vec_ref[0:1, :] + vec_ref[1:2, :]).astype(bf16)
    for number, row in ((0, 2), (1, None), (2, 3)):
        lane = (number % 2) * D
        weight = full_ref[:, number // 2, :, lane : lane + D].reshape(D, D)
        part = mm(first_in, weight)
        if row is not None:
            part = part + vec_ref[row : row + 1, :]
        qkv_ref[number] = part.astype(bf16).T
    fill_bias(seg_ref, bias_ref)

    def one_head(head, carry):
        rows = pl.ds(pl.multiple_of(head * HEAD_DIM, HEAD_DIM), HEAD_DIM)
        for blk in range(TOK // QBLK):
            cols = slice(blk * QBLK, (blk + 1) * QBLK)
            keys = (blk + 1) * QBLK
            query = qkv_ref[0, rows, cols] * bf16(HEAD_DIM**-0.5)
            scores = mm_tn(qkv_ref[1, rows, :keys], query) + bias_ref[:keys, cols]
            top = jnp.max(scores, axis=0, keepdims=True)
            e = jnp.exp(scores - top)
            total = jnp.sum(e, axis=0, keepdims=True)
            probs = (e * (1.0 / total)).astype(bf16)
            mixed_ref[rows, cols] = mm(qkv_ref[2, rows, :keys], probs).astype(bf16)
            lse_ref[pl.ds(head, 1), :, cols] = (top + jnp.log(total)).reshape(1, 1, QBLK)
        return carry

    lax.fori_loop(0, HEADS, one_head, 0, unroll=True)
    out_weight = full_ref[:, 1, :, D:].reshape(D, D)
    resid_ref[...] = hidden + (mm_tn(mixed_ref[...], out_weight) + vec_ref[4:5, :])


def mlp_step(plan, cuts, *refs):
    n = plan.n_opt - 1
    stream = plan.mlp
    resid_ref, cot_ref, seg_ref, vec_ref, bup_ref, own_ref = refs[:6]
    pieces = [refs[6 + n * k : 6 + n * (k + 1)] for k in range(2 * cuts)]
    outs, send_ref = refs[6 + 2 * cuts * n : -1], refs[-1]
    keep_ref, sends = outs[0], outs[1 : 1 + stream.places]
    act_ref, dres_ref, gvec_ref, gbup_ref, full_ref, out_acc, db_acc = outs[1 + stream.places :]
    assemble(plan, own_ref, pieces[:cuts], pieces[cuts:], full_ref)
    core, ybit = position()[:2]
    resid = resid_ref[...]
    normed, rstd = ln_parts(resid)
    second_in = (normed * vec_ref[5:6, :] + vec_ref[6:7, :]).astype(bf16)
    second_t = second_in.T
    dy = jnp.where(column_of(seg_ref[...]) >= 0, cot_ref[...].astype(f32), 0.0)
    dy_low = dy.astype(bf16)
    dy_t = dy_low.T
    out_acc[...] = jnp.zeros_like(out_acc)
    db_acc[...] = jnp.zeros_like(db_acc)
    wide = FF // 2

    def one_block(blk, carry):
        cols = pl.ds(pl.multiple_of(blk * wide, wide), wide)
        up = full_ref[:, 0, :, cols].reshape(D, wide)
        down = full_ref[:, 1, :, cols].reshape(D, wide)
        pre = mm(second_in, up) + bup_ref[blk]
        sq = pre * pre
        th = jnp.tanh(gelu_c * pre * (1.0 + 0.044715 * sq))
        half = 0.5 * (1.0 + th)
        act = (pre * half).astype(bf16)
        slope = half + (0.5 * gelu_c) * pre * (1.0 - th * th) * (1.0 + (3 * 0.044715) * sq)
        out_acc[...] += mm_nt(act, down)
        dpre = (mm(dy_low, down) * slope).astype(bf16)
        gbup_ref[blk] = jnp.sum(dpre.astype(f32), axis=0, keepdims=True)
        db_acc[...] += mm_nt(dpre, up)
        base = (blk ^ ybit) * (stream.total // 2)
        for mat, (left, right) in enumerate(((second_t, dpre), (dy_t, act))):
            grad = mm(left, right)
            first, last = grad[:, :D], grad[:, D:]
            store_chunks(plan, stream, keep_ref, base, jnp.where(core == 0, first, last), mat)
            store_chunks(plan, stream, send_ref, base, jnp.where(core == 0, last, first), mat)
        return carry

    lax.fori_loop(0, 2, one_block, 0, unroll=True)
    split_sends(stream, send_ref, sends)
    act_ref[...] = (resid + out_acc[...] + vec_ref[7:8, :]).astype(bf16)
    db = db_acc[...]
    dres_ref[...] = dy + ln_back(db, vec_ref[5:6, :], normed, rstd)
    gvec_ref[0:1, :] = jnp.sum(db * normed, axis=0, keepdims=True)
    gvec_ref[1:2, :] = jnp.sum(db, axis=0, keepdims=True)
    gvec_ref[2:3, :] = jnp.sum(dy, axis=0, keepdims=True)
    gvec_ref[3:8, :] = jnp.zeros((5, D), f32)


def back_heads(first, last, qkv_ref, bias_ref, lse_ref, dmix_ref, dqkv_ref, dkv_acc):
    scale = HEAD_DIM**-0.5
    for head in range(first, last):
        rows = slice(head * HEAD_DIM, (head + 1) * HEAD_DIM)
        out_rows = slice((head - first) * HEAD_DIM, (head - first + 1) * HEAD_DIM)
        for blk in range(TOK // QBLK):
            cols = slice(blk * QBLK, (blk + 1) * QBLK)
            keys = (blk + 1) * QBLK
            query = qkv_ref[0, rows, cols]
            key = qkv_ref[1, rows, :keys]
            value = qkv_ref[2, rows, :keys]
            dmix = dmix_ref[rows, cols]
            scores = mm_tn(key, query * bf16(scale)) + bias_ref[:keys, cols]
            probs = jnp.exp(scores - lse_ref[head][:, cols])
            dprobs = mm_tn(value, dmix)
            row_dot = jnp.sum(probs * dprobs, axis=0, keepdims=True)
            dscores = (probs * (dprobs - row_dot)).astype(bf16)
            dqkv_ref[0, out_rows, cols] = (mm(key, dscores) * scale).astype(bf16)
            dkey = mm_nt(query, dscores)
            dvalue = mm_nt(dmix, probs.astype(bf16))
            if blk == 0:
                dkv_acc[0, :, :QBLK] = dkey
                dkv_acc[1, :, :QBLK] = dvalue
            else:
                dkv_acc[0, :, :QBLK] += dkey[:, :QBLK]
                dkv_acc[1, :, :QBLK] += dvalue[:, :QBLK]
                dkv_acc[0, :, QBLK:] = dkey[:, QBLK:]
                dkv_acc[1, :, QBLK:] = dvalue[:, QBLK:]
        dqkv_ref[1, out_rows, :] = (dkv_acc[0] * scale).astype(bf16)
        dqkv_ref[2, out_rows, :] = dkv_acc[1].astype(bf16)


def attn_back_first(last, seg_ref, dres_ref, full_ref, mixed_ref, qkv_ref, lse_ref,
                    dmix_ref, gout_ref, gbo_ref, dqkv_ref, bias_ref, dkv_acc):
    dz = dres_ref[...].astype(bf16)
    gbo_ref[...] = jnp.broadcast_to(jnp.sum(dz.astype(f32), axis=0, keepdims=True), (8, D))
    out_weight = full_ref[:, 1, :, D:].reshape(D, D)
    dmix_ref[...] = mm_nt(out_weight, dz).astype(bf16)
    gout_ref[...] = mm(mixed_ref[...], dz)
    fill_bias(seg_ref, bias_ref)
    back_heads(0, last, qkv_ref, bias_ref, lse_ref, dmix_ref, dqkv_ref, dkv_acc)


def attn_back_next(first, last, seg_ref, dmix_ref, qkv_ref, lse_ref, *refs):
    sources, dqkv_ref, states, (bias_ref, dkv_acc, sems) = refs[:6], refs[6], refs[7:13], refs[13:]
    copies = [pltpu.make_async_copy(src, dst, sems.at[k]) for k, (src, dst) in enumerate(zip(sources, states))]
    for copy in copies:
        copy.start()
    fill_bias(seg_ref, bias_ref)
    back_heads(first, last, qkv_ref, bias_ref, lse_ref, dmix_ref, dqkv_ref, dkv_acc)
    for copy in copies:
        copy.wait()


def attn_back_last(plan, count, *refs):
    stream = plan.attn
    tok_ref, dres_ref, full_ref, vec_ref, gout_ref, gbo_ref, gvec_ref, gbup_ref = refs[:8]
    parts = refs[8 : 8 + count]
    keep_ref, sends = refs[8 + count], refs[9 + count : 9 + count + stream.places]
    tail_ref, igrad_ref, send_ref = refs[9 + count + stream.places :]
    core, ybit = position()[:2]
    hidden = tok_ref[...].astype(f32)
    normed, rstd = ln_parts(hidden)
    first_in = (normed * vec_ref[0:1, :] + vec_ref[1:2, :]).astype(bf16)
    first_t = first_in.T
    dqkv = [jnp.concatenate([part[number] for part in parts], axis=0) for number in range(3)]
    grads = [mm_nt(first_t, dpart) for dpart in dqkv] + [gout_ref[...]]
    for pair in range(2):
        base = (pair ^ ybit) * (stream.total // 2)
        first, last = grads[2 * pair], grads[2 * pair + 1]
        store_chunks(plan, stream, keep_ref, base, jnp.where(core == 0, first, last), 0)
        store_chunks(plan, stream, send_ref, base, jnp.where(core == 0, last, first), 0)
    split_sends(stream, send_ref, sends)
    da_t = jnp.zeros((D, TOK), f32)
    for number in range(3):
        lane = (number % 2) * D
        weight = full_ref[:, number // 2, :, lane : lane + D].reshape(D, D)
        da_t = da_t + mm(weight, dqkv[number])
    da = da_t.T
    igrad_ref[...] = dres_ref[...] + ln_back(da, vec_ref[0:1, :], normed, rstd)
    ones = jnp.ones((8, TOK), bf16)
    rows = [
        jnp.sum(da * normed, axis=0, keepdims=True),
        jnp.sum(da, axis=0, keepdims=True),
        mm_nt(ones, dqkv[0])[0:1, :],
        mm_nt(ones, dqkv[2])[0:1, :],
        gbo_ref[0:1, :],
        gvec_ref[0:3, :],
    ]
    for blk in range(2):
        rows += [gbup_ref[blk][:, :D], gbup_ref[blk][:, D:]]
    rows.append(jnp.zeros((VEC_ROWS - 12, D), f32))
    total = jnp.concatenate(rows, axis=0)
    for t in range(stream.tail):
        piece = total[t * stream.unit : (t + 1) * stream.unit]
        keep_ref[stream.total + t] = piece
        tail_ref[t] = piece.astype(bf16)


def add_core(stream, keep_ref, *refs):
    others, outs = refs[: -stream.places], refs[-stream.places :]
    size = stream.piece
    for number in range(stream.places):
        total = keep_ref[number * size : (number + 1) * size] + others[number][...].astype(f32)
        outs[number][:size] = total.astype(outs[number].dtype)
    if stream.tail:
        total = keep_ref[stream.total :] + others[stream.places][...].astype(f32)
        for number in range(stream.places):
            outs[number][size:] = total.astype(outs[number].dtype)


def add_plane(stream, keep_ref, *refs):
    others, outs = refs[: -stream.split], refs[-stream.split :]
    size = outs[0].shape[0]
    for number, out in enumerate(outs):
        part = slice(number * size, (number + 1) * size)
        total = keep_ref[part]
        for other in others:
            total = total + other[part].astype(f32)
        out[...] = total.astype(out.dtype)


def add_two(left_ref, right_ref, *outs):
    total = left_ref[...].astype(f32) + right_ref[...].astype(f32)
    size = outs[0].shape[0]
    outs[0][...] = total[:size].astype(outs[0].dtype)
    if len(outs) > 1:
        outs[1][...] = total[size:]


def add_last(plan, stream, left_ref, right_ref, w_ref, m_ref, v_ref, out_ref, nw_ref, nm_ref, nv_ref, sum_ref):
    out_ref[...] = (left_ref[: stream.shard].astype(f32) + right_ref[: stream.shard].astype(f32)).astype(bf16)
    total = left_ref[stream.shard :].astype(f32) + right_ref[stream.shard :].astype(f32)
    sum_ref[...] = total.reshape(VEC_ROWS, D)
    op = position()[3]
    count = w_ref.shape[0] // D
    for k in range(count):
        grad = sum_ref[pl.ds(op * count + k, 1), :].reshape(D)
        here = slice(k * D, (k + 1) * D)
        out = adamw(w_ref[here], m_ref[here], v_ref[here], grad, vector_rate, 0.0)
        nw_ref[here], nm_ref[here], nv_ref[here] = out


def swap_core(n_dp, value):
    return lax.ppermute(value, "dp", [(i, i ^ 1) for i in range(n_dp)])


def swap_dp(plan, value, mask):
    return lax.ppermute(value, "dp", [(i, i ^ mask) for i in range(plan.n_dp)])


def reduce_core(plan, stream, keep, sends):
    got = [swap_core(plan.n_dp, send) for send in sends]
    shape = (stream.piece + stream.tail, stream.unit, D)
    outs = [shaped(shape, f32 if k == 0 else bf16) for k in range(stream.places)]

    def finish(got):
        return call(
            functools.partial(add_core, stream),
            outs,
            [vmem] * (1 + len(got)),
            [keep, *got],
            name="add_core_" + stream.name,
        )

    return got, finish


def send_plane(plan, parts):
    n_dp, n_opt = plan.n_dp, plan.n_opt
    got = []
    for number in range(1, 2 * n_opt):
        mask_y, mask_o = number // n_opt, number % n_opt
        perm = [
            ((d * n_opt + o), ((d ^ (2 * mask_y)) * n_opt + (o ^ mask_o))) for d in range(n_dp) for o in range(n_opt)
        ]
        got.append(lax.ppermute(parts[number], ("dp", "opt"), perm))
    return got


def reduce_plane(stream, keep, got):
    size = (stream.piece + stream.tail) // stream.split
    first = f32 if stream.split > 1 else bf16
    outs = [shaped((size, stream.unit, D), first if k == 0 else bf16) for k in range(stream.split)]
    return call(
        functools.partial(add_plane, stream),
        outs,
        [vmem] * (1 + len(got)),
        [keep, *got],
        name="add_plane_" + stream.name,
    )


def reduce_pair(stream, left, right, last=False):
    shapes = [shaped(left.shape, bf16)]
    if last and stream.tail:
        shapes = [shaped((stream.shard, stream.unit, D), bf16), shaped((stream.tail, stream.unit, D), f32)]
    return call(add_two, shapes, [vmem] * 2, [left, right], name="add_two_" + stream.name)


def adamw(weight, first, second, grad, rate, decay):
    first = beta_one * first + (1.0 - beta_one) * grad
    second = beta_two * second + (1.0 - beta_two) * grad * grad
    first_hat = first * (1.0 / (1.0 - beta_one**STEP))
    second_hat = second * (1.0 / (1.0 - beta_two**STEP))
    root = second_hat * lax.rsqrt(second_hat)
    weight = weight - rate * (first_hat / (root + adam_eps) + decay * weight)
    return weight, first, second


def adam_kernel(stream, rows, *refs):
    count = 4 * stream.split
    grads = refs[:count]
    w_ref, m_ref, v_ref, nw_ref, nm_ref, nv_ref = refs[count:]
    mat, part = pl.program_id(0), pl.program_id(1)
    core, ybit, zi, _ = position()
    place = core + 2 * ybit
    cuts = stream.chunk // rows
    zrel = (part // cuts) ^ (zi & (stream.split - 1))
    for z in range(stream.split):

        @pl.when(zrel == z)
        def _(z=z):
            for number in range(4):
                ref = grads[z * 4 + number]
                cols = pl.ds(pl.multiple_of((number ^ place) * D, D), D)
                for step in range(rows // stream.unit):
                    at = mat * stream.per + (part % cuts) * (rows // stream.unit) + step
                    here = (slice(step * stream.unit, (step + 1) * stream.unit), cols)
                    grad = ref[at].astype(f32)
                    out = adamw(w_ref[here], m_ref[here], v_ref[here], grad, matrix_rate, matrix_decay)
                    nw_ref[here], nm_ref[here], nv_ref[here] = out


def adam_matrix(plan, stream, grads, weight, first, second):
    rows = min(stream.chunk, ROWS)
    block = pl.BlockSpec((rows, 4 * D), lambda i, k: (k, i))
    shape = shaped(weight.shape, f32)
    states = [weight, first, second]
    if HOLD:
        states = [pltpu.with_memory_space_constraint(x, pltpu.HBM) for x in states]
    return pl.pallas_call(
        functools.partial(adam_kernel, stream, rows),
        grid=(stream.mats, plan.own // rows),
        out_shape=[shape] * 3,
        in_specs=[vmem] * len(grads) + [block] * 3,
        out_specs=[block] * 3,
        compiler_params=pltpu.CompilerParams(vmem_limit_bytes=16 * MIB),
        cost_estimate=pl.CostEstimate(
            flops=16 * weight.size, bytes_accessed=24 * weight.size, transcendentals=weight.size
        ),
        name="adam_" + stream.name,
    )(*grads, *states)


def body(plan, tokens, segment, cotangent, w_attn, m_attn, v_attn, w_mlp, m_mlp, v_mlp, vectors, m_vec, v_vec):
    n_dp, n_opt, own = plan.n_dp, plan.n_opt, plan.own
    core = lax.axis_index("dp") & 1
    seg = segment.reshape(1, TOK)

    def spread(send):
        return [lax.ppermute(send, "opt", [(o, o ^ m) for o in range(n_opt)]) for m in range(1, n_opt)]

    width = 2 * D
    length = vectors.shape[0]
    vec_pad = jnp.pad(vectors.astype(bf16), (0, 16 * width - length)).reshape(16, width)
    attn_half = lax.dynamic_slice(w_attn, (0, core * width), (own, width)).astype(bf16)
    attn_send = jnp.concatenate([attn_half, vec_pad], axis=0)
    attn_direct = spread(attn_send)
    attn_cross = [swap_core(n_dp, piece) for piece in attn_direct]
    widths = MLP_CUT
    attn_low, mlp_low, *mlp_halves = call(
        functools.partial(cast_weights, plan),
        [shaped((own, 4 * D), bf16), shaped((own, 2 * FF), bf16)] + [shaped((own, w), bf16) for w in widths],
        [vmem] * 2,
        [w_attn, after(w_mlp, attn_send)],
        name="cast_weights",
        room=20,
    )
    mlp_direct = [spread(half) for k, half in enumerate(mlp_halves)]
    size = math.gcd(length, D)
    full, qkv, mixed, lse, resid, vec8, bup = call(
        functools.partial(attn_forward, plan, length),
        [
            shaped((n_opt, 2, own, width), bf16),
            shaped((3, D, TOK), bf16),
            shaped((D, TOK), bf16),
            shaped((HEADS, 1, TOK), f32),
            shaped((TOK, D), f32),
            shaped((8, D), f32),
            shaped((2, 1, FF // 2), f32),
        ],
        [vmem] * (4 + 2 * (n_opt - 1)),
        [tokens, seg, attn_low, attn_send, *attn_direct, *attn_cross],
        [pltpu.VMEM((TOK, TOK), f32), pltpu.VMEM((n_opt * length // size, 1, size), f32)],
        flops=2 * TOK * D * 4 * D + 8 * TOK * TOK * D,
        name="attn_forward",
    )
    mlp_cross = [[swap_core(n_dp, after(piece, resid)) for piece in pieces] for pieces in mlp_direct]
    stream = plan.mlp
    mlp_keep, *rest = call(
        functools.partial(mlp_step, plan, len(widths)),
        [
            shaped((stream.total, stream.unit, D), f32),
            *[shaped((stream.piece, stream.unit, D), bf16)] * stream.places,
            shaped((TOK, D), bf16),
            shaped((TOK, D), f32),
            shaped((8, D), f32),
            shaped((2, 1, FF // 2), f32),
        ],
        [vmem] * (6 + 2 * len(widths) * (n_opt - 1)),
        [resid, cotangent, seg, vec8, bup, mlp_low, *sum(mlp_direct, []), *sum(mlp_cross, [])],
        [
            pltpu.VMEM((n_opt, 2, own, FF), bf16),
            pltpu.VMEM((TOK, D), f32),
            pltpu.VMEM((TOK, D), f32),
            pltpu.VMEM((stream.total, stream.unit, D), bf16),
        ],
        flops=12 * TOK * D * FF,
        room=20,
        name="mlp_step",
    )
    mlp_sends, (activations, dres, gvec, gbup) = rest[: stream.places], rest[stream.places :]
    mlp_got, finish = reduce_core(plan, stream, mlp_keep, mlp_sends)

    head_flops = 14 * TOK * TOK * HEAD_DIM
    head_scratch = [pltpu.VMEM((TOK, TOK), f32), pltpu.VMEM((2, HEAD_DIM, TOK), f32)]
    cuts = (0, 2, 6)
    dmix, gout, gbo, part = call(
        functools.partial(attn_back_first, cuts[1]),
        [
            shaped((D, TOK), bf16),
            shaped((D, D), f32),
            shaped((8, D), f32),
            shaped((3, cuts[1] * HEAD_DIM, TOK), bf16),
        ],
        [vmem] * 6,
        [seg, dres, full, mixed, qkv, lse],
        head_scratch,
        flops=4 * TOK * D * D + cuts[1] * head_flops,
        name="attn_back_first",
    )
    mlp_got[0] = after(mlp_got[0], dmix)
    mlp_parts = finish(mlp_got)
    dmix = after(dmix, *mlp_parts)
    states = [w_mlp, m_mlp, v_mlp, w_attn, m_attn, v_attn]
    next_part, *states = call(
        functools.partial(attn_back_next, cuts[1], cuts[2]),
        [shaped((3, (cuts[2] - cuts[1]) * HEAD_DIM, TOK), bf16)] + [shaped(x.shape, f32) for x in states],
        [vmem] * 4 + [pl.BlockSpec(memory_space=pl.ANY)] * 6,
        [seg, dmix, qkv, lse] + [pltpu.with_memory_space_constraint(x, pltpu.HBM) for x in states],
        head_scratch + [pltpu.SemaphoreType.DMA((6,))],
        light=True,
        room=24,
        name="attn_back_next",
    )
    parts = [part, next_part]
    stream = plan.attn
    attn_keep, *attn_sends, input_grad = call(
        functools.partial(attn_back_last, plan, len(parts)),
        [
            shaped((stream.total + stream.tail, stream.unit, D), f32),
            *[shaped((stream.piece, stream.unit, D), bf16)] * stream.places,
            shaped((stream.tail, stream.unit, D), bf16),
            shaped((TOK, D), f32),
        ],
        [vmem] * (8 + len(parts)),
        [tokens, dres, full, vec8, gout, gbo, gvec, gbup, *parts],
        [pltpu.VMEM((stream.total, stream.unit, D), bf16)],
        light=True,
        flops=12 * TOK * D * D,
        name="attn_back_last",
    )
    mlp, attn = plan.mlp, plan.attn
    zbits = [4 << k for k in range(plan.n_z.bit_length() - 1)]
    attn_got, finish = reduce_core(plan, attn, attn_keep, attn_sends)
    mlp_got = send_plane(plan, mlp_parts)
    mlp_keep, mlp_send = reduce_plane(mlp, mlp_parts[0], mlp_got)
    attn_got[0] = after(attn_got[0], mlp_send)
    attn_parts = finish(attn_got)
    mlp_got = swap_dp(plan, mlp_send, zbits[0])
    attn_got = send_plane(plan, attn_parts)
    mlp_got = after(mlp_got, attn_parts[1])
    (mlp_own,) = reduce_pair(mlp, mlp_keep, mlp_got)
    mlp_got = swap_dp(plan, mlp_own, zbits[1])
    attn_got[0] = after(attn_got[0], mlp_own)
    (attn_own,) = reduce_plane(attn, attn_parts[0], attn_got)
    attn_got = swap_dp(plan, attn_own, zbits[0])
    mlp_got = after(mlp_got, attn_own)
    (mlp_own,) = reduce_pair(mlp, mlp_own, mlp_got)
    for mask in zbits[2:]:
        (mlp_own,) = reduce_pair(mlp, mlp_own, swap_dp(plan, mlp_own, mask))
    mlp_z = swap_dp(plan, mlp_own, zbits[0])
    mlp_y = swap_dp(plan, mlp_own, 2)
    attn_got = after(attn_got, mlp_own)
    (attn_own,) = reduce_pair(attn, attn_own, attn_got)
    for mask in zbits[2:]:
        (attn_own,) = reduce_pair(attn, attn_own, swap_dp(plan, attn_own, mask))
    attn_got = swap_dp(plan, attn_own, zbits[1])
    mlp_z = after(mlp_z, attn_own)
    mlp_yz = swap_dp(plan, mlp_z, 2)
    near = [mlp_own, mlp_y, mlp_z, mlp_yz]
    cross = [swap_core(n_dp, x) for x in near]
    mlp_grads = [near[0], cross[0], near[1], cross[1], near[2], cross[2], near[3], cross[3]]
    if length % D == 0:
        vec = shaped((length,), f32)
        attn_own, new_vec, first_vec, second_vec = call(
            functools.partial(add_last, plan, attn),
            [shaped((attn.shard, attn.unit, D), bf16), vec, vec, vec],
            [vmem] * 5,
            [attn_own, attn_got, vectors, m_vec, v_vec],
            [pltpu.VMEM((VEC_ROWS, D), f32)],
            name="add_last",
        )
    else:
        attn_own, vec_grad = reduce_pair(attn, attn_own, attn_got, last=True)
        own_vec = lax.dynamic_slice(vec_grad.reshape(-1), (lax.axis_index("opt") * length,), (length,))
        new_vec, first_vec, second_vec = adamw(vectors, m_vec, v_vec, own_vec, vector_rate, 0.0)
    attn_y = swap_dp(plan, attn_own, 2)
    mlp_grads[0] = after(mlp_grads[0], attn_own)
    new_mlp, first_mlp, second_mlp = adam_matrix(plan, mlp, mlp_grads, *states[:3])
    attn_y = after(attn_y, new_mlp)
    attn_grads = [attn_own, swap_core(n_dp, attn_own), attn_y, swap_core(n_dp, attn_y)]
    new_attn, first_attn, second_attn = adam_matrix(plan, attn, attn_grads, *states[3:])
    return (
        activations,
        input_grad,
        new_attn,
        first_attn,
        second_attn,
        new_mlp,
        first_mlp,
        second_mlp,
        new_vec,
        first_vec,
        second_vec,
    )


def solution(mesh):
    rows, both = P("opt", None), P(("dp", "opt"), None)
    in_specs = (both, P(("dp", "opt")), both) + (rows,) * 6 + (P("opt"),) * 3
    out_specs = (both, both) + (rows,) * 6 + (P("opt"),) * 3
    return jax.shard_map(
        functools.partial(body, Plan(mesh)), mesh=mesh, in_specs=in_specs, out_specs=out_specs, check_vma=False
    )
```

```python
import functools
import math

import jax
import jax.numpy as jnp
from jax import lax
from jax.experimental import pallas as pl
from jax.experimental.pallas import tpu as pltpu
from jax.sharding import PartitionSpec as P

D = 384
HEADS = 6
HEAD_DIM = 64
FF = 1536
TOK = 512
QBLK = 256
STEP = 10
VEC_ROWS = 16

norm_eps = 1e-05
beta_one = 0.9
beta_two = 0.95
adam_eps = 1e-08
matrix_rate = 0.15
vector_rate = 0.6
matrix_decay = 0.1
neg_large = -1e30
gelu_c = math.sqrt(2.0 / math.pi)

f32 = jnp.float32
bf16 = jnp.bfloat16
MIB = 1024 * 1024
HOLD = False
ROWS = 96
WIDE = FF // 2
EARLY = 384

vmem = pl.BlockSpec(memory_space=pltpu.VMEM)


def dot(left, right, dims):
    return lax.dot_general(left, right, ((dims[:1], dims[1:]), ((), ())), preferred_element_type=f32)


def mm(left, right):
    return dot(left, right, (1, 0))


def mm_nt(left, right):
    return dot(left, right, (1, 1))


def mm_tn(left, right):
    return dot(left, right, (0, 0))


def ln_parts(values):
    mean = jnp.mean(values, axis=-1, keepdims=True)
    centred = values - mean
    var = jnp.mean(centred * centred, axis=-1, keepdims=True)
    rstd = lax.rsqrt(var + norm_eps)
    return centred * rstd, rstd


def ln_back(grad, gain, normed, rstd):
    e = grad * gain
    mean_e = jnp.mean(e, axis=-1, keepdims=True)
    mean_en = jnp.mean(e * normed, axis=-1, keepdims=True)
    return (e - mean_e - normed * mean_en) * rstd


def after(value, *others):
    return lax.optimization_barrier((value, *others))[0]


def call(kernel, outs, ins, args, scratch=(), flops=0, name=None, room=12, light=False):
    moved = sum(math.prod(a.shape) * a.dtype.itemsize for a in args)
    moved += sum(math.prod(o.shape) * o.dtype.itemsize for o in outs)
    return pl.pallas_call(
        kernel,
        out_shape=list(outs),
        in_specs=list(ins),
        out_specs=[vmem] * len(outs),
        scratch_shapes=list(scratch),
        compiler_params=pltpu.CompilerParams(vmem_limit_bytes=room * MIB),
        cost_estimate=pl.CostEstimate(
            flops=0 if light else flops, bytes_accessed=0 if light else moved, transcendentals=0
        ),
        name=name,
    )(*args)


def shaped(shape, dtype):
    return jax.ShapeDtypeStruct(shape, dtype)


class Plan:
    def __init__(self, mesh):
        self.n_dp = mesh.shape["dp"]
        self.n_opt = mesh.shape["opt"]
        self.n_z = self.n_dp // 4
        self.own = D // self.n_opt
        self.attn = Stream(self, "attn", 1, 1, VEC_ROWS)
        self.mlp = Stream(self, "mlp", 2, 2, 0)


class Stream:
    def __init__(self, plan, name, mats, split, tail):
        self.name, self.mats, self.split = name, mats, split
        self.chunk = plan.own // split
        self.unit = math.gcd(self.chunk, 16)
        self.per = self.chunk // self.unit
        self.tail = tail // self.unit
        self.shard = mats * self.per
        self.places = 2 * plan.n_opt
        self.piece = split * self.shard
        self.total = self.places * self.piece


def position():
    dp, op = lax.axis_index("dp"), lax.axis_index("opt")
    return dp & 1, (dp >> 1) & 1, dp >> 2, op


def assemble(plan, own_halves, messages, full_ref):
    core, _, _, op = position()
    for half, value in enumerate(own_halves):
        full_ref[op, half] = value
    for cols, direct, cross in messages:
        for half, pieces in ((core, direct), (1 - core, cross)):
            for m in range(1, plan.n_opt):
                full_ref[op ^ m, half, :, cols] = pieces[m - 1][...]


def assemble_quarters(plan, own_ref, pieces, full_ref):
    core, ybit, _, op = position()
    for half in range(2):
        full_ref[op, half] = own_ref[:, half * 2 * D : (half + 1) * 2 * D]
    for rel, messages in pieces.items():
        cols = pl.ds(pl.multiple_of((ybit ^ (rel // 2)) * D, D), D)
        for m in range(1, plan.n_opt):
            full_ref[op ^ m, core ^ (rel % 2), :, cols] = messages[m - 1][: plan.own, :]


def store_chunks(plan, stream, ref, base, value, mat):
    _, _, zi, op = position()
    for i in range(plan.n_opt * stream.split):
        rel = ((i // stream.split) ^ op) * stream.split + ((i % stream.split) ^ (zi & (stream.split - 1)))
        for t in range(stream.per):
            row = i * stream.chunk + t * stream.unit
            at = base + (rel * stream.mats + mat) * stream.per + t
            ref[at] = value[row : row + stream.unit].astype(ref.dtype)


def split_sends(stream, whole_ref, refs):
    for number, ref in enumerate(refs):
        ref[: stream.piece] = whole_ref[number * stream.piece : (number + 1) * stream.piece]


def column_of(row):
    return jnp.broadcast_to(row.astype(f32), (8, TOK)).T[:, :1]


def fill_bias(seg_ref, bias_ref):
    key = lax.broadcasted_iota(jnp.int32, (TOK, TOK), 0)
    query = lax.broadcasted_iota(jnp.int32, (TOK, TOK), 1)
    seg_query = seg_ref[...].astype(f32)
    allowed = (column_of(seg_ref[...]) == seg_query) & (key <= query) & ((seg_query >= 0) | (key == query))
    bias_ref[...] = jnp.where(allowed, 0.0, neg_large)


def spread_vec(plan, length, own_ref, direct, piece_ref, vec_ref, bup_ref):
    _, _, _, op = position()
    size = piece_ref.shape[2]
    count, width = length // size, own_ref.shape[1]
    for m in range(plan.n_opt):
        ref = own_ref if m == 0 else direct[m - 1]
        rows = ref[plan.own : plan.own + 16, :].astype(f32)
        for k in range(count):
            row, lane = (k * size) // width, (k * size) % width
            piece_ref[(op ^ m) * count + k] = rows[row : row + 1, lane : lane + size]
    per = D // size

    def row_of(number):
        return jnp.concatenate([piece_ref[number * per + k] for k in range(per)], axis=1)

    for number in range(8):
        vec_ref[number : number + 1, :] = row_of(number)
    for blk in range(2):
        bup_ref[blk] = jnp.concatenate([row_of(8 + 2 * blk), row_of(9 + 2 * blk)], axis=1)


def cast_weights(plan, attn_ref, mlp_ref, attn_low, mlp_low, early_ref, late_ref):
    core, ybit = position()[:2]
    attn_low[...] = attn_ref[...].astype(bf16)
    mlp_low[...] = mlp_ref[...].astype(bf16)
    far = pl.multiple_of(core * FF + (ybit ^ 1) * WIDE, 128)
    near = pl.multiple_of(core * FF + ybit * WIDE, 128)
    early_ref[:, :WIDE] = mlp_low[:, pl.ds(far, WIDE)]
    early_ref[:, WIDE:] = mlp_low[:, pl.ds(near, EARLY)]
    late_ref[...] = mlp_low[:, pl.ds(near + EARLY, WIDE - EARLY)]


def first_message(plan, w_ref, vec_ref, send_ref, part_ref, low_ref, sems):
    core, ybit = position()[:2]
    start = pl.multiple_of((2 * core + ybit) * D, D)
    copies = [
        pltpu.make_async_copy(w_ref.at[:, pl.ds(start, D)], part_ref, sems.at[0]),
        pltpu.make_async_copy(vec_ref, low_ref, sems.at[1]),
    ]
    for copy in copies:
        copy.start()
    copies[1].wait()
    if len(low_ref.shape) == 1:
        rows = low_ref.shape[0] // D
        pieces = [low_ref[k * D : (k + 1) * D].reshape(1, D) for k in range(rows)]
        pieces.append(jnp.zeros((16 - rows, D), f32))
        send_ref[plan.own :, :] = jnp.concatenate(pieces, axis=0).astype(bf16)
    else:
        send_ref[plan.own :, :] = low_ref[...].astype(bf16)
    copies[0].wait()
    send_ref[: plan.own, :] = part_ref[...].astype(bf16)


def forward_heads(first, last, qkv_ref, bias_ref, mixed_ref, lse_ref):
    for head in range(first, last):
        rows = slice(head * HEAD_DIM, (head + 1) * HEAD_DIM)
        for blk in range(TOK // QBLK):
            cols = slice(blk * QBLK, (blk + 1) * QBLK)
            keys = (blk + 1) * QBLK
            query = qkv_ref[0, rows, cols] * bf16(HEAD_DIM**-0.5)
            scores = mm_tn(qkv_ref[1, rows, :keys], query) + bias_ref[:keys, cols]
            top = jnp.max(scores, axis=0, keepdims=True)
            e = jnp.exp(scores - top)
            total = jnp.sum(e, axis=0, keepdims=True)
            probs = (e * (1.0 / total)).astype(bf16)
            mixed_ref[rows, cols] = mm(qkv_ref[2, rows, :keys], probs).astype(bf16)
            lse_ref[head, :, cols] = top + jnp.log(total)


def attn_enter(plan, length, heads, *refs):
    n = plan.n_opt - 1
    tok_ref, seg_ref, own_ref, sent_ref = refs[:4]
    pieces = {rel: refs[4 + n * rel : 4 + n * (rel + 1)] for rel in range(4)}
    full_ref, qkv_ref, mixed_ref, lse_ref, bias_ref, vec_ref, bup_ref, piece_ref = refs[4 + 4 * n :]
    assemble_quarters(plan, own_ref, pieces, full_ref)
    spread_vec(plan, length, sent_ref, pieces[0], piece_ref, vec_ref, bup_ref)
    normed, _ = ln_parts(tok_ref[...].astype(f32))
    first_in = (normed * vec_ref[0:1, :] + vec_ref[1:2, :]).astype(bf16)
    for number, row in ((0, 2), (1, None), (2, 3)):
        lane = (number % 2) * D
        weight = full_ref[:, number // 2, :, lane : lane + D].reshape(D, D)
        part = mm(first_in, weight)
        if row is not None:
            part = part + vec_ref[row : row + 1, :]
        qkv_ref[number] = part.astype(bf16).T
    fill_bias(seg_ref, bias_ref)
    forward_heads(0, heads, qkv_ref, bias_ref, mixed_ref, lse_ref)


def attn_leave(heads, tok_ref, full_ref, qkv_ref, mixed_in, lse_in, bias_ref, vec_ref, mixed_ref, lse_ref, resid_ref):
    mixed_ref[: heads * HEAD_DIM] = mixed_in[...]
    lse_ref[:heads] = lse_in[...]
    forward_heads(heads, HEADS, qkv_ref, bias_ref, mixed_ref, lse_ref)
    out_weight = full_ref[:, 1, :, D:].reshape(D, D)
    resid_ref[...] = tok_ref[...].astype(f32) + (mm_tn(mixed_ref[...], out_weight) + vec_ref[4:5, :])


def mlp_block(plan, rel, *refs):
    n = plan.n_opt - 1
    stream = plan.mlp
    resid_ref, cot_ref, seg_ref, vec_ref, bup_ref, own_ref = refs[:6]
    direct, cross, refs = refs[6 : 6 + n], refs[6 + n : 6 + 2 * n], refs[6 + 2 * n :]
    messages = [(slice(0, WIDE), [r.at[:, :WIDE] for r in direct], [r.at[:, :WIDE] for r in cross])]
    out_part, db_part = None, None
    if rel == 0:
        messages = [
            (slice(0, EARLY), [r.at[:, WIDE:] for r in direct], [r.at[:, WIDE:] for r in cross]),
            (slice(EARLY, WIDE), refs[:n], refs[n : 2 * n]),
        ]
        out_part, db_part, refs = refs[2 * n], refs[2 * n + 1], refs[2 * n + 2 :]
    keep_ref, sends = refs[0], refs[1 : 1 + plan.n_opt]
    gbup_ref, refs = refs[1 + plan.n_opt], refs[2 + plan.n_opt :]
    core, ybit = position()[:2]
    blk = ybit ^ rel
    full_ref, send_ref = refs[-2:]
    halves = [own_ref[:, pl.ds(pl.multiple_of(mat * FF + blk * WIDE, 128), WIDE)] for mat in range(2)]
    assemble(plan, halves, messages, full_ref)
    up, down = full_ref[:, 0].reshape(D, WIDE), full_ref[:, 1].reshape(D, WIDE)
    resid = resid_ref[...]
    normed, rstd = ln_parts(resid)
    second_in = (normed * vec_ref[5:6, :] + vec_ref[6:7, :]).astype(bf16)
    dy = jnp.where(column_of(seg_ref[...]) >= 0, cot_ref[...].astype(f32), 0.0)
    dy_low = dy.astype(bf16)
    pre = mm(second_in, up) + bup_ref[blk]
    sq = pre * pre
    th = jnp.tanh(gelu_c * pre * (1.0 + 0.044715 * sq))
    half = 0.5 * (1.0 + th)
    act = (pre * half).astype(bf16)
    slope = half + (0.5 * gelu_c) * pre * (1.0 - th * th) * (1.0 + (3 * 0.044715) * sq)
    dpre = (mm(dy_low, down) * slope).astype(bf16)
    gbup_ref[...] = jnp.sum(dpre.astype(f32), axis=0, keepdims=True)
    for mat, (left, right) in enumerate(((second_in.T, dpre), (dy_low.T, act))):
        grad = mm(left, right)
        first, last = grad[:, :D], grad[:, D:]
        store_chunks(plan, stream, keep_ref, 0, jnp.where(core == 0, first, last), mat)
        store_chunks(plan, stream, send_ref, 0, jnp.where(core == 0, last, first), mat)
    split_sends(stream, send_ref, sends)
    out, db = mm_nt(act, down), mm_nt(dpre, up)
    if rel == 1:
        refs[0][...], refs[1][...] = out, db
        return
    act_ref, dres_ref, gvec_ref = refs[:3]
    act_ref[...] = (resid + (out_part[...] + out) + vec_ref[7:8, :]).astype(bf16)
    db = db_part[...] + db
    dres_ref[...] = dy + ln_back(db, vec_ref[5:6, :], normed, rstd)
    gvec_ref[0:1, :] = jnp.sum(db * normed, axis=0, keepdims=True)
    gvec_ref[1:2, :] = jnp.sum(db, axis=0, keepdims=True)
    gvec_ref[2:3, :] = jnp.sum(dy, axis=0, keepdims=True)
    gvec_ref[3:8, :] = jnp.zeros((5, D), f32)


def back_heads(first, last, qkv_ref, bias_ref, lse_ref, dmix_ref, dqkv_ref, dkv_acc):
    scale = HEAD_DIM**-0.5
    for head in range(first, last):
        rows = slice(head * HEAD_DIM, (head + 1) * HEAD_DIM)
        out_rows = slice((head - first) * HEAD_DIM, (head - first + 1) * HEAD_DIM)
        for blk in range(TOK // QBLK):
            cols = slice(blk * QBLK, (blk + 1) * QBLK)
            keys = (blk + 1) * QBLK
            query = qkv_ref[0, rows, cols]
            key = qkv_ref[1, rows, :keys]
            value = qkv_ref[2, rows, :keys]
            dmix = dmix_ref[rows, cols]
            scores = mm_tn(key, query * bf16(scale)) + bias_ref[:keys, cols]
            probs = jnp.exp(scores - lse_ref[head][:, cols])
            dprobs = mm_tn(value, dmix)
            row_dot = jnp.sum(probs * dprobs, axis=0, keepdims=True)
            dscores = (probs * (dprobs - row_dot)).astype(bf16)
            dqkv_ref[0, out_rows, cols] = (mm(key, dscores) * scale).astype(bf16)
            dkey = mm_nt(query, dscores)
            dvalue = mm_nt(dmix, probs.astype(bf16))
            if blk == 0:
                dkv_acc[0, :, :QBLK] = dkey
                dkv_acc[1, :, :QBLK] = dvalue
            else:
                dkv_acc[0, :, :QBLK] += dkey[:, :QBLK]
                dkv_acc[1, :, :QBLK] += dvalue[:, :QBLK]
                dkv_acc[0, :, QBLK:] = dkey[:, QBLK:]
                dkv_acc[1, :, QBLK:] = dvalue[:, QBLK:]
        dqkv_ref[1, out_rows, :] = (dkv_acc[0] * scale).astype(bf16)
        dqkv_ref[2, out_rows, :] = dkv_acc[1].astype(bf16)


def start_loads(sources, targets, sems):
    copies = [pltpu.make_async_copy(src, dst, sems.at[k]) for k, (src, dst) in enumerate(zip(sources, targets))]
    for copy in copies:
        copy.start()
    return copies


def attn_back_first(last, bias_ref, dres_ref, full_ref, mixed_ref, qkv_ref, lse_ref, *refs):
    sources, (dmix_ref, gout_ref, gbo_ref, dqkv_ref), states = refs[:3], refs[3:7], refs[7:10]
    dkv_acc, sems = refs[10:]
    copies = start_loads(sources, states, sems)
    dz = dres_ref[...].astype(bf16)
    gbo_ref[...] = jnp.broadcast_to(jnp.sum(dz.astype(f32), axis=0, keepdims=True), (8, D))
    out_weight = full_ref[:, 1, :, D:].reshape(D, D)
    dmix_ref[...] = mm_nt(out_weight, dz).astype(bf16)
    gout_ref[...] = mm(mixed_ref[...], dz)
    back_heads(0, last, qkv_ref, bias_ref, lse_ref, dmix_ref, dqkv_ref, dkv_acc)
    for copy in copies:
        copy.wait()


def attn_back_next(first, last, bias_ref, dmix_ref, qkv_ref, lse_ref, *refs):
    sources, dqkv_ref, states, (dkv_acc, sems) = refs[:3], refs[3], refs[4:7], refs[7:]
    copies = start_loads(sources, states, sems)
    back_heads(first, last, qkv_ref, bias_ref, lse_ref, dmix_ref, dqkv_ref, dkv_acc)
    for copy in copies:
        copy.wait()


def attn_back_last(plan, count, *refs):
    stream = plan.attn
    tok_ref, dres_ref, full_ref, vec_ref, gout_ref, gbo_ref, gvec_ref, gbup0, gbup1 = refs[:9]
    parts = refs[9 : 9 + count]
    keep_ref, sends = refs[9 + count], refs[10 + count : 10 + count + stream.places]
    igrad_ref, send_ref = refs[10 + count + stream.places :]
    core, ybit = position()[:2]
    hidden = tok_ref[...].astype(f32)
    normed, rstd = ln_parts(hidden)
    first_in = (normed * vec_ref[0:1, :] + vec_ref[1:2, :]).astype(bf16)
    first_t = first_in.T
    dqkv = [jnp.concatenate([part[number] for part in parts], axis=0) for number in range(3)]
    grads = [mm_nt(first_t, dpart) for dpart in dqkv] + [gout_ref[...]]
    for pair in range(2):
        base = (pair ^ ybit) * (stream.total // 2)
        first, last = grads[2 * pair], grads[2 * pair + 1]
        store_chunks(plan, stream, keep_ref, base, jnp.where(core == 0, first, last), 0)
        store_chunks(plan, stream, send_ref, base, jnp.where(core == 0, last, first), 0)
    split_sends(stream, send_ref, sends)
    da_t = jnp.zeros((D, TOK), f32)
    for number in range(3):
        lane = (number % 2) * D
        weight = full_ref[:, number // 2, :, lane : lane + D].reshape(D, D)
        da_t = da_t + mm(weight, dqkv[number])
    da = da_t.T
    igrad_ref[...] = dres_ref[...] + ln_back(da, vec_ref[0:1, :], normed, rstd)
    ones = jnp.ones((8, TOK), bf16)
    rows = [
        jnp.sum(da * normed, axis=0, keepdims=True),
        jnp.sum(da, axis=0, keepdims=True),
        mm_nt(ones, dqkv[0])[0:1, :],
        mm_nt(ones, dqkv[2])[0:1, :],
        gbo_ref[0:1, :],
        gvec_ref[0:3, :],
    ]
    for blk in range(2):
        near, far = (gbup0, gbup1) if blk == 0 else (gbup1, gbup0)
        gbup = jnp.where(ybit == 0, near[...], far[...])
        rows += [gbup[:, :D], gbup[:, D:]]
    rows.append(jnp.zeros((VEC_ROWS - 12, D), f32))
    total = jnp.concatenate(rows, axis=0)
    for t in range(stream.tail):
        piece = total[t * stream.unit : (t + 1) * stream.unit]
        keep_ref[stream.total + t] = piece
        sends[-1][stream.piece + t] = piece.astype(bf16)


def add_core(stream, count, keep_ref, *refs):
    others, outs = refs[:-count], refs[-count:]
    size = stream.piece
    for number in range(count):
        total = keep_ref[number * size : (number + 1) * size] + others[number][:size].astype(f32)
        outs[number][:size] = total.astype(outs[number].dtype)
    if stream.tail:
        total = keep_ref[count * size :] + others[-1][size:].astype(f32)
        for number in range(count):
            outs[number][size:] = total.astype(outs[number].dtype)


def add_plane(stream, keep_ref, *refs):
    others, outs = refs[: -stream.split], refs[-stream.split :]
    size = outs[0].shape[0]
    for number, out in enumerate(outs):
        part = slice(number * size, (number + 1) * size)
        total = keep_ref[part]
        for other in others:
            total = total + other[part].astype(f32)
        out[...] = total.astype(out.dtype)


def add_two(left_ref, right_ref, *outs):
    total = left_ref[...].astype(f32) + right_ref[...].astype(f32)
    size = outs[0].shape[0]
    outs[0][...] = total[:size].astype(outs[0].dtype)
    if len(outs) > 1:
        outs[1][...] = total[size:]


def add_last(plan, stream, left_ref, right_ref, w_ref, m_ref, v_ref, out_ref, nw_ref, nm_ref, nv_ref, sum_ref):
    out_ref[...] = (left_ref[: stream.shard].astype(f32) + right_ref[: stream.shard].astype(f32)).astype(bf16)
    total = left_ref[stream.shard :].astype(f32) + right_ref[stream.shard :].astype(f32)
    sum_ref[...] = total.reshape(VEC_ROWS, D)
    op = position()[3]
    count = w_ref.shape[0] // D
    for k in range(count):
        grad = sum_ref[pl.ds(op * count + k, 1), :].reshape(D)
        here = slice(k * D, (k + 1) * D)
        out = adamw(w_ref[here], m_ref[here], v_ref[here], grad, vector_rate, 0.0)
        nw_ref[here], nm_ref[here], nv_ref[here] = out


def swap_core(n_dp, value):
    return lax.ppermute(value, "dp", [(i, i ^ 1) for i in range(n_dp)])


def swap_dp(plan, value, mask):
    return lax.ppermute(value, "dp", [(i, i ^ mask) for i in range(plan.n_dp)])


def reduce_core(stream, keep, got, keeps_first, count):
    shape = (stream.piece + stream.tail, stream.unit, D)
    outs = [shaped(shape, f32 if k == 0 and keeps_first else bf16) for k in range(count)]
    return call(
        functools.partial(add_core, stream, count),
        outs,
        [vmem] * (1 + len(got)),
        [keep, *got],
        name="add_core_" + stream.name,
    )


def send_plane(plan, parts):
    n_dp, n_opt = plan.n_dp, plan.n_opt
    got = []
    for number in range(1, 2 * n_opt):
        mask_y, mask_o = number // n_opt, number % n_opt
        perm = [
            ((d * n_opt + o), ((d ^ (2 * mask_y)) * n_opt + (o ^ mask_o))) for d in range(n_dp) for o in range(n_opt)
        ]
        got.append(lax.ppermute(parts[number], ("dp", "opt"), perm))
    return got


def reduce_plane(stream, keep, got):
    size = (stream.piece + stream.tail) // stream.split
    first = f32 if stream.split > 1 else bf16
    outs = [shaped((size, stream.unit, D), first if k == 0 else bf16) for k in range(stream.split)]
    return call(
        functools.partial(add_plane, stream),
        outs,
        [vmem] * (1 + len(got)),
        [keep, *got],
        name="add_plane_" + stream.name,
    )


def reduce_pair(stream, left, right, last=False):
    shapes = [shaped(left.shape, bf16)]
    if last and stream.tail:
        shapes = [shaped((stream.shard, stream.unit, D), bf16), shaped((stream.tail, stream.unit, D), f32)]
    return call(add_two, shapes, [vmem] * 2, [left, right], name="add_two_" + stream.name)


def adamw(weight, first, second, grad, rate, decay):
    first = beta_one * first + (1.0 - beta_one) * grad
    second = beta_two * second + (1.0 - beta_two) * grad * grad
    first_hat = first * (1.0 / (1.0 - beta_one**STEP))
    second_hat = second * (1.0 / (1.0 - beta_two**STEP))
    root = second_hat * lax.rsqrt(second_hat)
    weight = weight - rate * (first_hat / (root + adam_eps) + decay * weight)
    return weight, first, second


def adam_kernel(stream, rows, *refs):
    count = 4 * stream.split
    grads = refs[:count]
    w_ref, m_ref, v_ref, nw_ref, nm_ref, nv_ref = refs[count:]
    mat, part = pl.program_id(0), pl.program_id(1)
    core, ybit, zi, _ = position()
    place = core + 2 * ybit
    cuts = stream.chunk // rows
    zrel = (part // cuts) ^ (zi & (stream.split - 1))
    for z in range(stream.split):

        @pl.when(zrel == z)
        def _(z=z):
            for number in range(4):
                ref = grads[z * 4 + number]
                cols = pl.ds(pl.multiple_of((number ^ place) * D, D), D)
                for step in range(rows // stream.unit):
                    at = mat * stream.per + (part % cuts) * (rows // stream.unit) + step
                    here = (slice(step * stream.unit, (step + 1) * stream.unit), cols)
                    grad = ref[at].astype(f32)
                    out = adamw(w_ref[here], m_ref[here], v_ref[here], grad, matrix_rate, matrix_decay)
                    nw_ref[here], nm_ref[here], nv_ref[here] = out


def adam_matrix(plan, stream, grads, weight, first, second):
    rows = min(stream.chunk, ROWS)
    block = pl.BlockSpec((rows, 4 * D), lambda i, k: (k, i))
    shape = shaped(weight.shape, f32)
    states = [weight, first, second]
    if HOLD:
        states = [pltpu.with_memory_space_constraint(x, pltpu.HBM) for x in states]
    return pl.pallas_call(
        functools.partial(adam_kernel, stream, rows),
        grid=(stream.mats, plan.own // rows),
        out_shape=[shape] * 3,
        in_specs=[vmem] * len(grads) + [block] * 3,
        out_specs=[block] * 3,
        compiler_params=pltpu.CompilerParams(vmem_limit_bytes=16 * MIB),
        cost_estimate=pl.CostEstimate(
            flops=16 * weight.size, bytes_accessed=24 * weight.size, transcendentals=weight.size
        ),
        name="adam_" + stream.name,
    )(*grads, *states)


def body(plan, tokens, segment, cotangent, w_attn, m_attn, v_attn, w_mlp, m_mlp, v_mlp, vectors, m_vec, v_vec):
    n_dp, n_opt, own = plan.n_dp, plan.n_opt, plan.own
    seg = segment.reshape(1, TOK)

    def spread(send):
        return [lax.ppermute(send, "opt", [(o, o ^ m) for o in range(n_opt)]) for m in range(1, n_opt)]

    any_spec = pl.BlockSpec(memory_space=pl.ANY)
    length = vectors.shape[0]
    vec_in = vectors if length % D == 0 else jnp.pad(vectors, (0, 16 * D - length)).reshape(16, D)
    (attn_send,) = call(
        functools.partial(first_message, plan),
        [shaped((own + 16, D), bf16)],
        [any_spec] * 2,
        [pltpu.with_memory_space_constraint(x, pltpu.HBM) for x in (w_attn, vec_in)],
        [pltpu.VMEM((own, D), f32), pltpu.VMEM(vec_in.shape, f32), pltpu.SemaphoreType.DMA((2,))],
        light=True,
        name="first_message",
    )
    attn_direct = spread(attn_send)
    attn_low, mlp_low, mlp_early, mlp_late = call(
        functools.partial(cast_weights, plan),
        [
            shaped((own, 4 * D), bf16),
            shaped((own, 2 * FF), bf16),
            shaped((own, WIDE + EARLY), bf16),
            shaped((own, WIDE - EARLY), bf16),
        ],
        [vmem] * 2,
        [w_attn, after(w_mlp, attn_send)],
        name="cast_weights",
        room=20,
    )
    early, late = spread(mlp_early), spread(mlp_late)
    attn_y = [swap_dp(plan, piece, 2) for piece in attn_direct]
    attn_pieces = attn_direct + [swap_core(n_dp, x) for x in attn_direct] + attn_y + [swap_core(n_dp, x) for x in attn_y]
    size = math.gcd(length, D)
    heads = 2
    full, qkv, mixed, lse, bias, vec8, bup = call(
        functools.partial(attn_enter, plan, length, heads),
        [
            shaped((n_opt, 2, own, 2 * D), bf16),
            shaped((3, D, TOK), bf16),
            shaped((heads * HEAD_DIM, TOK), bf16),
            shaped((heads, 1, TOK), f32),
            shaped((TOK, TOK), f32),
            shaped((8, D), f32),
            shaped((2, 1, FF // 2), f32),
        ],
        [vmem] * (4 + 4 * (n_opt - 1)),
        [tokens, seg, attn_low, attn_send, *attn_pieces],
        [pltpu.VMEM((n_opt * length // size, 1, size), f32)],
        flops=2 * TOK * D * 4 * D + 8 * TOK * TOK * D,
        light=True,
        name="attn_enter",
    )
    early += [swap_core(n_dp, after(piece, vec8)) for piece in early]
    mixed, lse, resid = call(
        functools.partial(attn_leave, heads),
        [shaped((D, TOK), bf16), shaped((HEADS, 1, TOK), f32), shaped((TOK, D), f32)],
        [vmem] * 7,
        [tokens, full, qkv, mixed, lse, bias, vec8],
        light=True,
        name="attn_leave",
    )
    stream = plan.mlp
    half_units = stream.total // 2
    half_outs = [
        shaped((half_units, stream.unit, D), f32),
        *[shaped((stream.piece, stream.unit, D), bf16)] * n_opt,
        shaped((1, WIDE), f32),
    ]
    half_scratch = [pltpu.VMEM((n_opt, 2, own, WIDE), bf16), pltpu.VMEM((half_units, stream.unit, D), bf16)]
    common = [resid, cotangent, seg, vec8, bup, mlp_low, *early]
    far_keep, *far_sends, gbup1, out_part, db_part = call(
        functools.partial(mlp_block, plan, 1),
        half_outs + [shaped((TOK, D), f32)] * 2,
        [vmem] * (6 + 2 * (n_opt - 1)),
        common,
        half_scratch,
        flops=6 * TOK * D * FF,
        room=20,
        light=True,
        name="mlp_far",
    )
    far_got = [swap_core(n_dp, send) for send in far_sends]
    late += [swap_core(n_dp, after(piece, out_part)) for piece in late]
    near_keep, *near_sends, gbup0, activations, dres, gvec = call(
        functools.partial(mlp_block, plan, 0),
        half_outs + [shaped((TOK, D), bf16), shaped((TOK, D), f32), shaped((8, D), f32)],
        [vmem] * (8 + 4 * (n_opt - 1)),
        common + late + [out_part, db_part],
        half_scratch,
        flops=6 * TOK * D * FF,
        room=20,
        name="mlp_near",
    )
    near_got = [swap_core(n_dp, send) for send in near_sends]
    far_got[0] = after(far_got[0], dres)
    far_parts = reduce_core(stream, far_keep, far_got, False, n_opt)
    dres_in = after(dres, *far_parts)

    head_flops = 14 * TOK * TOK * HEAD_DIM
    head_scratch = [pltpu.VMEM((2, HEAD_DIM, TOK), f32)]
    cuts = (0, 2, 6)
    head_scratch.append(pltpu.SemaphoreType.DMA((3,)))

    def state_args(arrays):
        return [pltpu.with_memory_space_constraint(x, pltpu.HBM) for x in arrays], [shaped(x.shape, f32) for x in arrays]

    sources, shapes = state_args([w_attn, m_attn, v_attn])
    dmix, gout, gbo, part, *attn_states = call(
        functools.partial(attn_back_first, cuts[1]),
        [
            shaped((D, TOK), bf16),
            shaped((D, D), f32),
            shaped((8, D), f32),
            shaped((3, cuts[1] * HEAD_DIM, TOK), bf16),
            *shapes,
        ],
        [vmem] * 6 + [any_spec] * 3,
        [bias, dres_in, full, mixed, qkv, lse, *sources],
        head_scratch,
        light=True,
        flops=4 * TOK * D * D + cuts[1] * head_flops,
        name="attn_back_first",
    )
    near_got[0] = after(near_got[0], dmix)
    mlp_parts = reduce_core(plan.mlp, near_keep, near_got, True, n_opt)
    dmix = after(dmix, *mlp_parts)
    sources, shapes = state_args([w_mlp, m_mlp, v_mlp])
    next_part, *mlp_states = call(
        functools.partial(attn_back_next, cuts[1], cuts[2]),
        [shaped((3, (cuts[2] - cuts[1]) * HEAD_DIM, TOK), bf16), *shapes],
        [vmem] * 4 + [any_spec] * 3,
        [bias, dmix, qkv, lse, *sources],
        head_scratch,
        light=True,
        room=20,
        name="attn_back_next",
    )
    parts = [part, next_part]
    stream = plan.attn
    attn_keep, *attn_sends, input_grad = call(
        functools.partial(attn_back_last, plan, len(parts)),
        [
            shaped((stream.total + stream.tail, stream.unit, D), f32),
            *[shaped((stream.piece, stream.unit, D), bf16)] * (stream.places - 1),
            shaped((stream.piece + stream.tail, stream.unit, D), bf16),
            shaped((TOK, D), f32),
        ],
        [vmem] * (9 + len(parts)),
        [tokens, dres, full, vec8, gout, gbo, gvec, gbup0, gbup1, *parts],
        [pltpu.VMEM((stream.total, stream.unit, D), bf16)],
        light=True,
        flops=12 * TOK * D * D,
        name="attn_back_last",
    )
    mlp, attn = plan.mlp, plan.attn
    zbits = [4 << k for k in range(plan.n_z.bit_length() - 1)]
    attn_got = [swap_core(n_dp, send) for send in attn_sends]
    mlp_got = send_plane(plan, mlp_parts + far_parts)
    mlp_keep, mlp_send = reduce_plane(mlp, mlp_parts[0], mlp_got)
    attn_got[0] = after(attn_got[0], mlp_send)
    attn_parts = reduce_core(attn, attn_keep, attn_got, True, attn.places)
    mlp_got = swap_dp(plan, mlp_send, zbits[0])
    attn_got = send_plane(plan, attn_parts)
    mlp_got = after(mlp_got, attn_parts[1])
    (mlp_own,) = reduce_pair(mlp, mlp_keep, mlp_got)
    mlp_got = swap_dp(plan, mlp_own, zbits[1])
    attn_got[0] = after(attn_got[0], mlp_own)
    (attn_own,) = reduce_plane(attn, attn_parts[0], attn_got)
    attn_got = swap_dp(plan, attn_own, zbits[0])
    mlp_got = after(mlp_got, attn_own)
    (mlp_own,) = reduce_pair(mlp, mlp_own, mlp_got)
    for mask in zbits[2:]:
        (mlp_own,) = reduce_pair(mlp, mlp_own, swap_dp(plan, mlp_own, mask))
    mlp_z = swap_dp(plan, mlp_own, zbits[0])
    mlp_y = swap_dp(plan, mlp_own, 2)
    attn_got = after(attn_got, mlp_own)
    (attn_own,) = reduce_pair(attn, attn_own, attn_got)
    for mask in zbits[2:]:
        (attn_own,) = reduce_pair(attn, attn_own, swap_dp(plan, attn_own, mask))
    attn_got = swap_dp(plan, attn_own, zbits[1])
    mlp_z = after(mlp_z, attn_own)
    mlp_yz = swap_dp(plan, mlp_z, 2)
    near = [mlp_own, mlp_y, mlp_z, mlp_yz]
    cross = [swap_core(n_dp, x) for x in near]
    mlp_grads = [near[0], cross[0], near[1], cross[1], near[2], cross[2], near[3], cross[3]]
    if length % D == 0:
        vec = shaped((length,), f32)
        attn_own, new_vec, first_vec, second_vec = call(
            functools.partial(add_last, plan, attn),
            [shaped((attn.shard, attn.unit, D), bf16), vec, vec, vec],
            [vmem] * 5,
            [attn_own, attn_got, vectors, m_vec, v_vec],
            [pltpu.VMEM((VEC_ROWS, D), f32)],
            name="add_last",
        )
    else:
        attn_own, vec_grad = reduce_pair(attn, attn_own, attn_got, last=True)
        own_vec = lax.dynamic_slice(vec_grad.reshape(-1), (lax.axis_index("opt") * length,), (length,))
        new_vec, first_vec, second_vec = adamw(vectors, m_vec, v_vec, own_vec, vector_rate, 0.0)
    attn_y = swap_dp(plan, attn_own, 2)
    mlp_grads[0] = after(mlp_grads[0], attn_own)
    new_mlp, first_mlp, second_mlp = adam_matrix(plan, mlp, mlp_grads, *mlp_states)
    attn_y = after(attn_y, new_mlp)
    attn_grads = [attn_own, swap_core(n_dp, attn_own), attn_y, swap_core(n_dp, attn_y)]
    new_attn, first_attn, second_attn = adam_matrix(plan, attn, attn_grads, *attn_states)
    return (
        activations,
        input_grad,
        new_attn,
        first_attn,
        second_attn,
        new_mlp,
        first_mlp,
        second_mlp,
        new_vec,
        first_vec,
        second_vec,
    )


def solution(mesh):
    rows, both = P("opt", None), P(("dp", "opt"), None)
    in_specs = (both, P(("dp", "opt")), both) + (rows,) * 6 + (P("opt"),) * 3
    out_specs = (both, both) + (rows,) * 6 + (P("opt"),) * 3
    return jax.shard_map(
        functools.partial(body, Plan(mesh)), mesh=mesh, in_specs=in_specs, out_specs=out_specs, check_vma=False
    )
```

```python
import functools
import math

import jax
import jax.numpy as jnp
from jax import lax
from jax.experimental import pallas as pl
from jax.experimental.pallas import tpu as pltpu
from jax.sharding import PartitionSpec as P

D = 384
HEADS = 6
HEAD_DIM = 64
FF = 1536
TOK = 512
QBLK = 256
FORWARD_BLK = 512
STEP = 10
VEC_ROWS = 16

norm_eps = 1e-05
beta_one = 0.9
beta_two = 0.95
adam_eps = 1e-08
matrix_rate = 0.15
vector_rate = 0.6
matrix_decay = 0.1
neg_large = -1e30
gelu_c = math.sqrt(2.0 / math.pi)

f32 = jnp.float32
bf16 = jnp.bfloat16
MIB = 1024 * 1024
HOLD = False
ROWS = 96
WIDE = FF // 2
EARLY = 384

vmem = pl.BlockSpec(memory_space=pltpu.VMEM)


def dot(left, right, dims):
    return lax.dot_general(left, right, ((dims[:1], dims[1:]), ((), ())), preferred_element_type=f32)


def mm(left, right):
    return dot(left, right, (1, 0))


def mm_nt(left, right):
    return dot(left, right, (1, 1))


def mm_tn(left, right):
    return dot(left, right, (0, 0))


def ln_parts(values):
    mean = jnp.mean(values, axis=-1, keepdims=True)
    centred = values - mean
    var = jnp.mean(centred * centred, axis=-1, keepdims=True)
    rstd = lax.rsqrt(var + norm_eps)
    return centred * rstd, rstd


def ln_back(grad, gain, normed, rstd):
    e = grad * gain
    mean_e = jnp.mean(e, axis=-1, keepdims=True)
    mean_en = jnp.mean(e * normed, axis=-1, keepdims=True)
    return (e - mean_e - normed * mean_en) * rstd


def after(value, *others):
    return lax.optimization_barrier((value, *others))[0]


def call(kernel, outs, ins, args, scratch=(), flops=0, name=None, room=12, light=False):
    moved = sum(math.prod(a.shape) * a.dtype.itemsize for a in args)
    moved += sum(math.prod(o.shape) * o.dtype.itemsize for o in outs)
    return pl.pallas_call(
        kernel,
        out_shape=list(outs),
        in_specs=list(ins),
        out_specs=[vmem] * len(outs),
        scratch_shapes=list(scratch),
        compiler_params=pltpu.CompilerParams(vmem_limit_bytes=room * MIB),
        cost_estimate=pl.CostEstimate(
            flops=0 if light else flops, bytes_accessed=0 if light else moved, transcendentals=0
        ),
        name=name,
    )(*args)


def shaped(shape, dtype):
    return jax.ShapeDtypeStruct(shape, dtype)


class Plan:
    def __init__(self, mesh):
        self.n_dp = mesh.shape["dp"]
        self.n_opt = mesh.shape["opt"]
        self.n_z = self.n_dp // 4
        self.own = D // self.n_opt
        self.attn = Stream(self, "attn", 1, 1, VEC_ROWS)
        self.mlp = Stream(self, "mlp", 2, 2, 0)


class Stream:
    def __init__(self, plan, name, mats, split, tail):
        self.name, self.mats, self.split = name, mats, split
        self.chunk = plan.own // split
        self.unit = math.gcd(self.chunk, 16)
        self.per = self.chunk // self.unit
        self.tail = tail // self.unit
        self.shard = mats * self.per
        self.places = 2 * plan.n_opt
        self.piece = split * self.shard
        self.total = self.places * self.piece


def position():
    dp, op = lax.axis_index("dp"), lax.axis_index("opt")
    return dp & 1, (dp >> 1) & 1, dp >> 2, op


def assemble(plan, own_halves, messages, full_ref):
    core, _, _, op = position()
    for half, value in enumerate(own_halves):
        full_ref[op, half] = value
    for cols, direct, cross in messages:
        for half, pieces in ((core, direct), (1 - core, cross)):
            for m in range(1, plan.n_opt):
                full_ref[op ^ m, half, :, cols] = pieces[m - 1][...]


def assemble_quarters(plan, own_ref, pieces, full_ref):
    core, ybit, _, op = position()
    for half in range(2):
        full_ref[op, half] = own_ref[:, half * 2 * D : (half + 1) * 2 * D]
    for rel, messages in pieces.items():
        cols = pl.ds(pl.multiple_of((ybit ^ (rel // 2)) * D, D), D)
        for m in range(1, plan.n_opt):
            full_ref[op ^ m, core ^ (rel % 2), :, cols] = messages[m - 1][: plan.own, :]


def store_chunks(plan, stream, ref, base, value, mat):
    _, _, zi, op = position()
    for i in range(plan.n_opt * stream.split):
        rel = ((i // stream.split) ^ op) * stream.split + ((i % stream.split) ^ (zi & (stream.split - 1)))
        for t in range(stream.per):
            row = i * stream.chunk + t * stream.unit
            at = base + (rel * stream.mats + mat) * stream.per + t
            ref[at] = value[row : row + stream.unit].astype(ref.dtype)


def split_sends(stream, whole_ref, refs):
    for number, ref in enumerate(refs):
        ref[: stream.piece] = whole_ref[number * stream.piece : (number + 1) * stream.piece]


def column_of(row):
    return jnp.broadcast_to(row.astype(f32), (8, TOK)).T[:, :1]


def fill_bias(seg_ref, bias_ref):
    key = lax.broadcasted_iota(jnp.int32, (TOK, TOK), 0)
    query = lax.broadcasted_iota(jnp.int32, (TOK, TOK), 1)
    seg_query = seg_ref[...].astype(f32)
    allowed = (column_of(seg_ref[...]) == seg_query) & (key <= query) & ((seg_query >= 0) | (key == query))
    bias_ref[...] = jnp.where(allowed, 0.0, neg_large)


def spread_vec(plan, length, own_ref, direct, piece_ref, vec_ref, bup_ref):
    _, _, _, op = position()
    size = piece_ref.shape[2]
    count, width = length // size, own_ref.shape[1]
    for m in range(plan.n_opt):
        ref = own_ref if m == 0 else direct[m - 1]
        rows = ref[plan.own : plan.own + 16, :].astype(f32)
        for k in range(count):
            row, lane = (k * size) // width, (k * size) % width
            piece_ref[(op ^ m) * count + k] = rows[row : row + 1, lane : lane + size]
    per = D // size

    def row_of(number):
        return jnp.concatenate([piece_ref[number * per + k] for k in range(per)], axis=1)

    for number in range(8):
        vec_ref[number : number + 1, :] = row_of(number)
    for blk in range(2):
        bup_ref[blk] = jnp.concatenate([row_of(8 + 2 * blk), row_of(9 + 2 * blk)], axis=1)


def cast_weights(plan, attn_ref, mlp_ref, attn_low, mlp_low, early_ref, late_ref):
    core, ybit = position()[:2]
    attn_low[...] = attn_ref[...].astype(bf16)
    mlp_low[...] = mlp_ref[...].astype(bf16)
    far = pl.multiple_of(core * FF + (ybit ^ 1) * WIDE, 128)
    near = pl.multiple_of(core * FF + ybit * WIDE, 128)
    early_ref[:, :WIDE] = mlp_low[:, pl.ds(far, WIDE)]
    early_ref[:, WIDE:] = mlp_low[:, pl.ds(near, EARLY)]
    late_ref[...] = mlp_low[:, pl.ds(near + EARLY, WIDE - EARLY)]


def first_message(plan, w_ref, vec_ref, send_ref, part_ref, low_ref, sems):
    core, ybit = position()[:2]
    start = pl.multiple_of((2 * core + ybit) * D, D)
    copies = [
        pltpu.make_async_copy(w_ref.at[:, pl.ds(start, D)], part_ref, sems.at[0]),
        pltpu.make_async_copy(vec_ref, low_ref, sems.at[1]),
    ]
    for copy in copies:
        copy.start()
    copies[1].wait()
    if len(low_ref.shape) == 1:
        rows = low_ref.shape[0] // D
        pieces = [low_ref[k * D : (k + 1) * D].reshape(1, D) for k in range(rows)]
        pieces.append(jnp.zeros((16 - rows, D), f32))
        send_ref[plan.own :, :] = jnp.concatenate(pieces, axis=0).astype(bf16)
    else:
        send_ref[plan.own :, :] = low_ref[...].astype(bf16)
    copies[0].wait()
    send_ref[: plan.own, :] = part_ref[...].astype(bf16)


def forward_heads(first, last, qkv_ref, bias_ref, mixed_ref, lse_ref):
    for head in range(first, last):
        rows = slice(head * HEAD_DIM, (head + 1) * HEAD_DIM)
        for blk in range(TOK // FORWARD_BLK):
            cols = slice(blk * FORWARD_BLK, (blk + 1) * FORWARD_BLK)
            keys = (blk + 1) * FORWARD_BLK
            query = qkv_ref[0, rows, cols] * bf16(HEAD_DIM**-0.5)
            scores = mm_tn(qkv_ref[1, rows, :keys], query) + bias_ref[:keys, cols]
            top = jnp.max(scores, axis=0, keepdims=True)
            e = jnp.exp(scores - top)
            total = jnp.sum(e, axis=0, keepdims=True)
            probs = (e * (1.0 / total)).astype(bf16)
            mixed_ref[rows, cols] = mm(qkv_ref[2, rows, :keys], probs).astype(bf16)
            lse_ref[head, :, cols] = top + jnp.log(total)


def attn_enter(plan, length, heads, *refs):
    n = plan.n_opt - 1
    tok_ref, seg_ref, own_ref, sent_ref = refs[:4]
    pieces = {rel: refs[4 + n * rel : 4 + n * (rel + 1)] for rel in range(4)}
    full_ref, qkv_ref, mixed_ref, lse_ref, bias_ref, vec_ref, bup_ref, piece_ref = refs[4 + 4 * n :]
    assemble_quarters(plan, own_ref, pieces, full_ref)
    spread_vec(plan, length, sent_ref, pieces[0], piece_ref, vec_ref, bup_ref)
    normed, _ = ln_parts(tok_ref[...].astype(f32))
    first_in = (normed * vec_ref[0:1, :] + vec_ref[1:2, :]).astype(bf16)
    for number, row in ((0, 2), (1, None), (2, 3)):
        lane = (number % 2) * D
        weight = full_ref[:, number // 2, :, lane : lane + D].reshape(D, D)
        part = mm(first_in, weight)
        if row is not None:
            part = part + vec_ref[row : row + 1, :]
        qkv_ref[number] = part.astype(bf16).T
    fill_bias(seg_ref, bias_ref)
    forward_heads(0, heads, qkv_ref, bias_ref, mixed_ref, lse_ref)


def attn_leave(heads, tok_ref, full_ref, qkv_ref, mixed_in, lse_in, bias_ref, vec_ref, mixed_ref, lse_ref, resid_ref):
    mixed_ref[: heads * HEAD_DIM] = mixed_in[...]
    lse_ref[:heads] = lse_in[...]
    forward_heads(heads, HEADS, qkv_ref, bias_ref, mixed_ref, lse_ref)
    out_weight = full_ref[:, 1, :, D:].reshape(D, D)
    resid_ref[...] = tok_ref[...].astype(f32) + (mm_tn(mixed_ref[...], out_weight) + vec_ref[4:5, :])


def mlp_block(plan, rel, *refs):
    n = plan.n_opt - 1
    stream = plan.mlp
    resid_ref, cot_ref, seg_ref, vec_ref, bup_ref, own_ref = refs[:6]
    direct, cross, refs = refs[6 : 6 + n], refs[6 + n : 6 + 2 * n], refs[6 + 2 * n :]
    messages = [(slice(0, WIDE), [r.at[:, :WIDE] for r in direct], [r.at[:, :WIDE] for r in cross])]
    out_part, db_part = None, None
    if rel == 0:
        messages = [
            (slice(0, EARLY), [r.at[:, WIDE:] for r in direct], [r.at[:, WIDE:] for r in cross]),
            (slice(EARLY, WIDE), refs[:n], refs[n : 2 * n]),
        ]
        out_part, db_part, refs = refs[2 * n], refs[2 * n + 1], refs[2 * n + 2 :]
    keep_ref, sends = refs[0], refs[1 : 1 + plan.n_opt]
    gbup_ref, refs = refs[1 + plan.n_opt], refs[2 + plan.n_opt :]
    core, ybit = position()[:2]
    blk = ybit ^ rel
    full_ref, send_ref = refs[-2:]
    halves = [own_ref[:, pl.ds(pl.multiple_of(mat * FF + blk * WIDE, 128), WIDE)] for mat in range(2)]
    assemble(plan, halves, messages, full_ref)
    up, down = full_ref[:, 0].reshape(D, WIDE), full_ref[:, 1].reshape(D, WIDE)
    resid = resid_ref[...]
    normed, rstd = ln_parts(resid)
    second_in = (normed * vec_ref[5:6, :] + vec_ref[6:7, :]).astype(bf16)
    dy = jnp.where(column_of(seg_ref[...]) >= 0, cot_ref[...].astype(f32), 0.0)
    dy_low = dy.astype(bf16)
    pre = mm(second_in, up) + bup_ref[blk]
    sq = pre * pre
    th = jnp.tanh(gelu_c * pre * (1.0 + 0.044715 * sq))
    half = 0.5 * (1.0 + th)
    act = (pre * half).astype(bf16)
    slope = half + (0.5 * gelu_c) * pre * (1.0 - th * th) * (1.0 + (3 * 0.044715) * sq)
    dpre = (mm(dy_low, down) * slope).astype(bf16)
    gbup_ref[...] = jnp.sum(dpre.astype(f32), axis=0, keepdims=True)
    for mat, (left, right) in enumerate(((second_in.T, dpre), (dy_low.T, act))):
        grad = mm(left, right)
        first, last = grad[:, :D], grad[:, D:]
        store_chunks(plan, stream, keep_ref, 0, jnp.where(core == 0, first, last), mat)
        store_chunks(plan, stream, send_ref, 0, jnp.where(core == 0, last, first), mat)
    split_sends(stream, send_ref, sends)
    out, db = mm_nt(act, down), mm_nt(dpre, up)
    if rel == 1:
        refs[0][...], refs[1][...] = out, db
        return
    act_ref, dres_ref, gvec_ref = refs[:3]
    act_ref[...] = (resid + (out_part[...] + out) + vec_ref[7:8, :]).astype(bf16)
    db = db_part[...] + db
    dres_ref[...] = dy + ln_back(db, vec_ref[5:6, :], normed, rstd)
    gvec_ref[0:1, :] = jnp.sum(db * normed, axis=0, keepdims=True)
    gvec_ref[1:2, :] = jnp.sum(db, axis=0, keepdims=True)
    gvec_ref[2:3, :] = jnp.sum(dy, axis=0, keepdims=True)
    gvec_ref[3:8, :] = jnp.zeros((5, D), f32)


def back_heads(first, last, qkv_ref, bias_ref, lse_ref, dmix_ref, dqkv_ref, dkv_acc):
    scale = HEAD_DIM**-0.5
    for head in range(first, last):
        rows = slice(head * HEAD_DIM, (head + 1) * HEAD_DIM)
        out_rows = slice((head - first) * HEAD_DIM, (head - first + 1) * HEAD_DIM)
        for blk in range(TOK // QBLK):
            cols = slice(blk * QBLK, (blk + 1) * QBLK)
            keys = (blk + 1) * QBLK
            query = qkv_ref[0, rows, cols]
            key = qkv_ref[1, rows, :keys]
            value = qkv_ref[2, rows, :keys]
            dmix = dmix_ref[rows, cols]
            scores = mm_tn(key, query * bf16(scale)) + bias_ref[:keys, cols]
            probs = jnp.exp(scores - lse_ref[head][:, cols])
            dprobs = mm_tn(value, dmix)
            row_dot = jnp.sum(probs * dprobs, axis=0, keepdims=True)
            dscores = (probs * (dprobs - row_dot)).astype(bf16)
            dqkv_ref[0, out_rows, cols] = (mm(key, dscores) * scale).astype(bf16)
            dkey = mm_nt(query, dscores)
            dvalue = mm_nt(dmix, probs.astype(bf16))
            if blk == 0:
                dkv_acc[0, :, :QBLK] = dkey
                dkv_acc[1, :, :QBLK] = dvalue
            else:
                dkv_acc[0, :, :QBLK] += dkey[:, :QBLK]
                dkv_acc[1, :, :QBLK] += dvalue[:, :QBLK]
                dkv_acc[0, :, QBLK:] = dkey[:, QBLK:]
                dkv_acc[1, :, QBLK:] = dvalue[:, QBLK:]
        dqkv_ref[1, out_rows, :] = (dkv_acc[0] * scale).astype(bf16)
        dqkv_ref[2, out_rows, :] = dkv_acc[1].astype(bf16)


def start_loads(sources, targets, sems):
    copies = [pltpu.make_async_copy(src, dst, sems.at[k]) for k, (src, dst) in enumerate(zip(sources, targets))]
    for copy in copies:
        copy.start()
    return copies


def attn_back_first(last, bias_ref, dres_ref, full_ref, mixed_ref, qkv_ref, lse_ref, *refs):
    sources, (dmix_ref, gout_ref, gbo_ref, dqkv_ref), states = refs[:3], refs[3:7], refs[7:10]
    dkv_acc, sems = refs[10:]
    copies = start_loads(sources, states, sems)
    dz = dres_ref[...].astype(bf16)
    gbo_ref[...] = jnp.broadcast_to(jnp.sum(dz.astype(f32), axis=0, keepdims=True), (8, D))
    out_weight = full_ref[:, 1, :, D:].reshape(D, D)
    dmix_ref[...] = mm_nt(out_weight, dz).astype(bf16)
    gout_ref[...] = mm(mixed_ref[...], dz)
    back_heads(0, last, qkv_ref, bias_ref, lse_ref, dmix_ref, dqkv_ref, dkv_acc)
    for copy in copies:
        copy.wait()


def attn_back_next(first, last, bias_ref, dmix_ref, qkv_ref, lse_ref, *refs):
    sources, dqkv_ref, states, (dkv_acc, sems) = refs[:3], refs[3], refs[4:7], refs[7:]
    copies = start_loads(sources, states, sems)
    back_heads(first, last, qkv_ref, bias_ref, lse_ref, dmix_ref, dqkv_ref, dkv_acc)
    for copy in copies:
        copy.wait()


def attn_back_last(plan, count, *refs):
    stream = plan.attn
    tok_ref, dres_ref, full_ref, vec_ref, gout_ref, gbo_ref, gvec_ref, gbup0, gbup1 = refs[:9]
    parts = refs[9 : 9 + count]
    keep_ref, sends = refs[9 + count], refs[10 + count : 10 + count + stream.places]
    igrad_ref, send_ref = refs[10 + count + stream.places :]
    core, ybit = position()[:2]
    hidden = tok_ref[...].astype(f32)
    normed, rstd = ln_parts(hidden)
    first_in = (normed * vec_ref[0:1, :] + vec_ref[1:2, :]).astype(bf16)
    first_t = first_in.T
    dqkv = [jnp.concatenate([part[number] for part in parts], axis=0) for number in range(3)]
    grads = [mm_nt(first_t, dpart) for dpart in dqkv] + [gout_ref[...]]
    for pair in range(2):
        base = (pair ^ ybit) * (stream.total // 2)
        first, last = grads[2 * pair], grads[2 * pair + 1]
        store_chunks(plan, stream, keep_ref, base, jnp.where(core == 0, first, last), 0)
        store_chunks(plan, stream, send_ref, base, jnp.where(core == 0, last, first), 0)
    split_sends(stream, send_ref, sends)
    da_t = jnp.zeros((D, TOK), f32)
    for number in range(3):
        lane = (number % 2) * D
        weight = full_ref[:, number // 2, :, lane : lane + D].reshape(D, D)
        da_t = da_t + mm(weight, dqkv[number])
    da = da_t.T
    igrad_ref[...] = dres_ref[...] + ln_back(da, vec_ref[0:1, :], normed, rstd)
    ones = jnp.ones((8, TOK), bf16)
    rows = [
        jnp.sum(da * normed, axis=0, keepdims=True),
        jnp.sum(da, axis=0, keepdims=True),
        mm_nt(ones, dqkv[0])[0:1, :],
        mm_nt(ones, dqkv[2])[0:1, :],
        gbo_ref[0:1, :],
        gvec_ref[0:3, :],
    ]
    for blk in range(2):
        near, far = (gbup0, gbup1) if blk == 0 else (gbup1, gbup0)
        gbup = jnp.where(ybit == 0, near[...], far[...])
        rows += [gbup[:, :D], gbup[:, D:]]
    rows.append(jnp.zeros((VEC_ROWS - 12, D), f32))
    total = jnp.concatenate(rows, axis=0)
    for t in range(stream.tail):
        piece = total[t * stream.unit : (t + 1) * stream.unit]
        keep_ref[stream.total + t] = piece
        sends[-1][stream.piece + t] = piece.astype(bf16)


def add_core(stream, count, keep_ref, *refs):
    others, outs = refs[:-count], refs[-count:]
    size = stream.piece
    for number in range(count):
        total = keep_ref[number * size : (number + 1) * size] + others[number][:size].astype(f32)
        outs[number][:size] = total.astype(outs[number].dtype)
    if stream.tail:
        total = keep_ref[count * size :] + others[-1][size:].astype(f32)
        for number in range(count):
            outs[number][size:] = total.astype(outs[number].dtype)


def add_plane(stream, keep_ref, *refs):
    others, outs = refs[: -stream.split], refs[-stream.split :]
    size = outs[0].shape[0]
    for number, out in enumerate(outs):
        part = slice(number * size, (number + 1) * size)
        total = keep_ref[part]
        for other in others:
            total = total + other[part].astype(f32)
        out[...] = total.astype(out.dtype)


def add_two(left_ref, right_ref, *outs):
    total = left_ref[...].astype(f32) + right_ref[...].astype(f32)
    size = outs[0].shape[0]
    outs[0][...] = total[:size].astype(outs[0].dtype)
    if len(outs) > 1:
        outs[1][...] = total[size:]


def add_last(plan, stream, left_ref, right_ref, w_ref, m_ref, v_ref, out_ref, nw_ref, nm_ref, nv_ref, sum_ref):
    out_ref[...] = (left_ref[: stream.shard].astype(f32) + right_ref[: stream.shard].astype(f32)).astype(bf16)
    total = left_ref[stream.shard :].astype(f32) + right_ref[stream.shard :].astype(f32)
    sum_ref[...] = total.reshape(VEC_ROWS, D)
    op = position()[3]
    count = w_ref.shape[0] // D
    for k in range(count):
        grad = sum_ref[pl.ds(op * count + k, 1), :].reshape(D)
        here = slice(k * D, (k + 1) * D)
        out = adamw(w_ref[here], m_ref[here], v_ref[here], grad, vector_rate, 0.0)
        nw_ref[here], nm_ref[here], nv_ref[here] = out


def swap_core(n_dp, value):
    return lax.ppermute(value, "dp", [(i, i ^ 1) for i in range(n_dp)])


def swap_dp(plan, value, mask):
    return lax.ppermute(value, "dp", [(i, i ^ mask) for i in range(plan.n_dp)])


def reduce_core(stream, keep, got, keeps_first, count):
    shape = (stream.piece + stream.tail, stream.unit, D)
    outs = [shaped(shape, f32 if k == 0 and keeps_first else bf16) for k in range(count)]
    return call(
        functools.partial(add_core, stream, count),
        outs,
        [vmem] * (1 + len(got)),
        [keep, *got],
        name="add_core_" + stream.name,
    )


def send_plane(plan, parts):
    n_dp, n_opt = plan.n_dp, plan.n_opt
    got = []
    for number in range(1, 2 * n_opt):
        mask_y, mask_o = number // n_opt, number % n_opt
        perm = [
            ((d * n_opt + o), ((d ^ (2 * mask_y)) * n_opt + (o ^ mask_o))) for d in range(n_dp) for o in range(n_opt)
        ]
        got.append(lax.ppermute(parts[number], ("dp", "opt"), perm))
    return got


def reduce_plane(stream, keep, got):
    size = (stream.piece + stream.tail) // stream.split
    first = f32 if stream.split > 1 else bf16
    outs = [shaped((size, stream.unit, D), first if k == 0 else bf16) for k in range(stream.split)]
    return call(
        functools.partial(add_plane, stream),
        outs,
        [vmem] * (1 + len(got)),
        [keep, *got],
        name="add_plane_" + stream.name,
    )


def reduce_pair(stream, left, right, last=False):
    shapes = [shaped(left.shape, bf16)]
    if last and stream.tail:
        shapes = [shaped((stream.shard, stream.unit, D), bf16), shaped((stream.tail, stream.unit, D), f32)]
    return call(add_two, shapes, [vmem] * 2, [left, right], name="add_two_" + stream.name)


def adamw(weight, first, second, grad, rate, decay):
    first = beta_one * first + (1.0 - beta_one) * grad
    second = beta_two * second + (1.0 - beta_two) * grad * grad
    first_hat = first * (1.0 / (1.0 - beta_one**STEP))
    second_hat = second * (1.0 / (1.0 - beta_two**STEP))
    root = second_hat * lax.rsqrt(second_hat)
    weight = weight - rate * (first_hat / (root + adam_eps) + decay * weight)
    return weight, first, second


def adam_kernel(stream, rows, *refs):
    count = 4 * stream.split
    grads = refs[:count]
    w_ref, m_ref, v_ref, nw_ref, nm_ref, nv_ref = refs[count:]
    mat, part = pl.program_id(0), pl.program_id(1)
    core, ybit, zi, _ = position()
    place = core + 2 * ybit
    cuts = stream.chunk // rows
    zrel = (part // cuts) ^ (zi & (stream.split - 1))
    for z in range(stream.split):

        @pl.when(zrel == z)
        def _(z=z):
            for number in range(4):
                ref = grads[z * 4 + number]
                cols = pl.ds(pl.multiple_of((number ^ place) * D, D), D)
                for step in range(rows // stream.unit):
                    at = mat * stream.per + (part % cuts) * (rows // stream.unit) + step
                    here = (slice(step * stream.unit, (step + 1) * stream.unit), cols)
                    grad = ref[at].astype(f32)
                    out = adamw(w_ref[here], m_ref[here], v_ref[here], grad, matrix_rate, matrix_decay)
                    nw_ref[here], nm_ref[here], nv_ref[here] = out


def adam_matrix(plan, stream, grads, weight, first, second):
    rows = min(stream.chunk, ROWS)
    block = pl.BlockSpec((rows, 4 * D), lambda i, k: (k, i))
    shape = shaped(weight.shape, f32)
    states = [weight, first, second]
    if HOLD:
        states = [pltpu.with_memory_space_constraint(x, pltpu.HBM) for x in states]
    return pl.pallas_call(
        functools.partial(adam_kernel, stream, rows),
        grid=(stream.mats, plan.own // rows),
        out_shape=[shape] * 3,
        in_specs=[vmem] * len(grads) + [block] * 3,
        out_specs=[block] * 3,
        compiler_params=pltpu.CompilerParams(vmem_limit_bytes=16 * MIB),
        cost_estimate=pl.CostEstimate(
            flops=16 * weight.size, bytes_accessed=24 * weight.size, transcendentals=weight.size
        ),
        name="adam_" + stream.name,
    )(*grads, *states)


def adam_half_kernel(stream, rel, *refs):
    grads, states, outs = refs[:2], refs[2:5], refs[-7:-4]
    bufs, sems = refs[-4:-1], refs[-1]
    core, ybit, _, _ = position()
    copies = []
    for number, ref in enumerate(grads):
        cols = pl.ds(pl.multiple_of(((number + 2 * rel) ^ (core + 2 * ybit)) * D, D), D)
        grad = ref[...].reshape(ref.shape[0] * ref.shape[1], D).astype(f32)
        values = adamw(*[state[:, cols] for state in states], grad, matrix_rate, matrix_decay)
        for k in range(3):
            bufs[k][number] = values[k]
            copy = pltpu.make_async_copy(bufs[k].at[number], outs[k].at[:, cols], sems.at[number, k])
            copy.start()
            copies.append(copy)
    for copy in copies:
        copy.wait()


def adam_half(plan, stream, rel, grads, states, before=()):
    any_spec = pl.BlockSpec(memory_space=pl.ANY)
    shape = shaped(states[0].shape, f32)
    return pl.pallas_call(
        functools.partial(adam_half_kernel, stream, rel),
        out_shape=[shape] * 3,
        in_specs=[vmem] * 5 + [any_spec] * len(before),
        out_specs=[any_spec] * 3,
        scratch_shapes=[pltpu.VMEM((2, plan.own, D), f32)] * 3 + [pltpu.SemaphoreType.DMA((2, 3))],
        input_output_aliases={5 + k: k for k in range(len(before))},
        compiler_params=pltpu.CompilerParams(vmem_limit_bytes=16 * MIB),
        cost_estimate=pl.CostEstimate(flops=0, bytes_accessed=0, transcendentals=0),
        name="adam_half_" + str(rel),
    )(*grads, *states, *before)


def body(plan, tokens, segment, cotangent, w_attn, m_attn, v_attn, w_mlp, m_mlp, v_mlp, vectors, m_vec, v_vec):
    n_dp, n_opt, own = plan.n_dp, plan.n_opt, plan.own
    seg = segment.reshape(1, TOK)

    def spread(send):
        return [lax.ppermute(send, "opt", [(o, o ^ m) for o in range(n_opt)]) for m in range(1, n_opt)]

    any_spec = pl.BlockSpec(memory_space=pl.ANY)
    length = vectors.shape[0]
    vec_in = vectors if length % D == 0 else jnp.pad(vectors, (0, 16 * D - length)).reshape(16, D)
    (attn_send,) = call(
        functools.partial(first_message, plan),
        [shaped((own + 16, D), bf16)],
        [any_spec] * 2,
        [pltpu.with_memory_space_constraint(x, pltpu.HBM) for x in (w_attn, vec_in)],
        [pltpu.VMEM((own, D), f32), pltpu.VMEM(vec_in.shape, f32), pltpu.SemaphoreType.DMA((2,))],
        light=True,
        name="first_message",
    )
    attn_direct = spread(attn_send)
    attn_low, mlp_low, mlp_early, mlp_late = call(
        functools.partial(cast_weights, plan),
        [
            shaped((own, 4 * D), bf16),
            shaped((own, 2 * FF), bf16),
            shaped((own, WIDE + EARLY), bf16),
            shaped((own, WIDE - EARLY), bf16),
        ],
        [vmem] * 2,
        [w_attn, after(w_mlp, attn_send)],
        name="cast_weights",
        room=20,
    )
    early, late = spread(mlp_early), spread(mlp_late)
    attn_y = [swap_dp(plan, piece, 2) for piece in attn_direct]
    attn_pieces = attn_direct + [swap_core(n_dp, x) for x in attn_direct] + attn_y + [swap_core(n_dp, x) for x in attn_y]
    size = math.gcd(length, D)
    heads = 2
    full, qkv, mixed, lse, bias, vec8, bup = call(
        functools.partial(attn_enter, plan, length, heads),
        [
            shaped((n_opt, 2, own, 2 * D), bf16),
            shaped((3, D, TOK), bf16),
            shaped((heads * HEAD_DIM, TOK), bf16),
            shaped((heads, 1, TOK), f32),
            shaped((TOK, TOK), f32),
            shaped((8, D), f32),
            shaped((2, 1, FF // 2), f32),
        ],
        [vmem] * (4 + 4 * (n_opt - 1)),
        [tokens, seg, attn_low, attn_send, *attn_pieces],
        [pltpu.VMEM((n_opt * length // size, 1, size), f32)],
        flops=2 * TOK * D * 4 * D + 8 * TOK * TOK * D,
        light=True,
        name="attn_enter",
    )
    early += [swap_core(n_dp, after(piece, vec8)) for piece in early]
    mixed, lse, resid = call(
        functools.partial(attn_leave, heads),
        [shaped((D, TOK), bf16), shaped((HEADS, 1, TOK), f32), shaped((TOK, D), f32)],
        [vmem] * 7,
        [tokens, full, qkv, mixed, lse, bias, vec8],
        light=True,
        name="attn_leave",
    )
    stream = plan.mlp
    half_units = stream.total // 2
    half_outs = [
        shaped((half_units, stream.unit, D), f32),
        *[shaped((stream.piece, stream.unit, D), bf16)] * n_opt,
        shaped((1, WIDE), f32),
    ]
    half_scratch = [pltpu.VMEM((n_opt, 2, own, WIDE), bf16), pltpu.VMEM((half_units, stream.unit, D), bf16)]
    common = [resid, cotangent, seg, vec8, bup, mlp_low, *early]
    far_keep, *far_sends, gbup1, out_part, db_part = call(
        functools.partial(mlp_block, plan, 1),
        half_outs + [shaped((TOK, D), f32)] * 2,
        [vmem] * (6 + 2 * (n_opt - 1)),
        common,
        half_scratch,
        flops=6 * TOK * D * FF,
        room=20,
        light=True,
        name="mlp_far",
    )
    far_got = [swap_core(n_dp, send) for send in far_sends]
    late += [swap_core(n_dp, after(piece, out_part)) for piece in late]
    near_keep, *near_sends, gbup0, activations, dres, gvec = call(
        functools.partial(mlp_block, plan, 0),
        half_outs + [shaped((TOK, D), bf16), shaped((TOK, D), f32), shaped((8, D), f32)],
        [vmem] * (8 + 4 * (n_opt - 1)),
        common + late + [out_part, db_part],
        half_scratch,
        flops=6 * TOK * D * FF,
        room=20,
        name="mlp_near",
    )
    near_got = [swap_core(n_dp, send) for send in near_sends]
    far_got[0] = after(far_got[0], dres)
    far_parts = reduce_core(stream, far_keep, far_got, False, n_opt)
    dres_in = after(dres, *far_parts)

    head_flops = 14 * TOK * TOK * HEAD_DIM
    head_scratch = [pltpu.VMEM((2, HEAD_DIM, TOK), f32)]
    cuts = (0, 2, 6)
    head_scratch.append(pltpu.SemaphoreType.DMA((3,)))

    def state_args(arrays):
        return [pltpu.with_memory_space_constraint(x, pltpu.HBM) for x in arrays], [shaped(x.shape, f32) for x in arrays]

    sources, shapes = state_args([w_attn, m_attn, v_attn])
    dmix, gout, gbo, part, *attn_states = call(
        functools.partial(attn_back_first, cuts[1]),
        [
            shaped((D, TOK), bf16),
            shaped((D, D), f32),
            shaped((8, D), f32),
            shaped((3, cuts[1] * HEAD_DIM, TOK), bf16),
            *shapes,
        ],
        [vmem] * 6 + [any_spec] * 3,
        [bias, dres_in, full, mixed, qkv, lse, *sources],
        head_scratch,
        light=True,
        flops=4 * TOK * D * D + cuts[1] * head_flops,
        name="attn_back_first",
    )
    near_got[0] = after(near_got[0], dmix)
    mlp_parts = reduce_core(plan.mlp, near_keep, near_got, True, n_opt)
    dmix = after(dmix, *mlp_parts)
    sources, shapes = state_args([w_mlp, m_mlp, v_mlp])
    next_part, *mlp_states = call(
        functools.partial(attn_back_next, cuts[1], cuts[2]),
        [shaped((3, (cuts[2] - cuts[1]) * HEAD_DIM, TOK), bf16), *shapes],
        [vmem] * 4 + [any_spec] * 3,
        [bias, dmix, qkv, lse, *sources],
        head_scratch,
        light=True,
        room=20,
        name="attn_back_next",
    )
    parts = [part, next_part]
    stream = plan.attn
    attn_keep, *attn_sends, input_grad = call(
        functools.partial(attn_back_last, plan, len(parts)),
        [
            shaped((stream.total + stream.tail, stream.unit, D), f32),
            *[shaped((stream.piece, stream.unit, D), bf16)] * (stream.places - 1),
            shaped((stream.piece + stream.tail, stream.unit, D), bf16),
            shaped((TOK, D), f32),
        ],
        [vmem] * (9 + len(parts)),
        [tokens, dres, full, vec8, gout, gbo, gvec, gbup0, gbup1, *parts],
        [pltpu.VMEM((stream.total, stream.unit, D), bf16)],
        light=True,
        flops=12 * TOK * D * D,
        name="attn_back_last",
    )
    mlp, attn = plan.mlp, plan.attn
    zbits = [4 << k for k in range(plan.n_z.bit_length() - 1)]
    attn_got = [swap_core(n_dp, send) for send in attn_sends]
    mlp_got = send_plane(plan, mlp_parts + far_parts)
    mlp_keep, mlp_send = reduce_plane(mlp, mlp_parts[0], mlp_got)
    attn_got[0] = after(attn_got[0], mlp_send)
    attn_parts = reduce_core(attn, attn_keep, attn_got, True, attn.places)
    mlp_got = swap_dp(plan, mlp_send, zbits[0])
    attn_got = send_plane(plan, attn_parts)
    mlp_got = after(mlp_got, attn_parts[1])
    (mlp_own,) = reduce_pair(mlp, mlp_keep, mlp_got)
    mlp_got = swap_dp(plan, mlp_own, zbits[1])
    attn_got[0] = after(attn_got[0], mlp_own)
    (attn_own,) = reduce_plane(attn, attn_parts[0], attn_got)
    attn_got = swap_dp(plan, attn_own, zbits[0])
    mlp_got = after(mlp_got, attn_own)
    (mlp_own,) = reduce_pair(mlp, mlp_own, mlp_got)
    for mask in zbits[2:]:
        (mlp_own,) = reduce_pair(mlp, mlp_own, swap_dp(plan, mlp_own, mask))
    mlp_z = swap_dp(plan, mlp_own, zbits[0])
    mlp_y = swap_dp(plan, mlp_own, 2)
    attn_got = after(attn_got, mlp_own)
    (attn_own,) = reduce_pair(attn, attn_own, attn_got)
    for mask in zbits[2:]:
        (attn_own,) = reduce_pair(attn, attn_own, swap_dp(plan, attn_own, mask))
    attn_got = swap_dp(plan, attn_own, zbits[1])
    mlp_z = after(mlp_z, attn_own)
    mlp_yz = swap_dp(plan, mlp_z, 2)
    near = [mlp_own, mlp_y, mlp_z, mlp_yz]
    cross = [swap_core(n_dp, x) for x in near]
    mlp_grads = [near[0], cross[0], near[1], cross[1], near[2], cross[2], near[3], cross[3]]
    if length % D == 0:
        vec = shaped((length,), f32)
        attn_own, new_vec, first_vec, second_vec = call(
            functools.partial(add_last, plan, attn),
            [shaped((attn.shard, attn.unit, D), bf16), vec, vec, vec],
            [vmem] * 5,
            [attn_own, attn_got, vectors, m_vec, v_vec],
            [pltpu.VMEM((VEC_ROWS, D), f32)],
            name="add_last",
        )
    else:
        attn_own, vec_grad = reduce_pair(attn, attn_own, attn_got, last=True)
        own_vec = lax.dynamic_slice(vec_grad.reshape(-1), (lax.axis_index("opt") * length,), (length,))
        new_vec, first_vec, second_vec = adamw(vectors, m_vec, v_vec, own_vec, vector_rate, 0.0)
    attn_y = swap_dp(plan, attn_own, 2)
    new_mlp, first_mlp, second_mlp = adam_matrix(plan, mlp, mlp_grads, *mlp_states)
    near_grads = [after(attn_own, new_mlp), swap_core(n_dp, attn_own)]
    near_done = adam_half(plan, attn, 0, near_grads, attn_states)
    attn_y = after(attn_y, new_mlp)
    cross_y = after(swap_core(n_dp, attn_y), near_done[0])
    new_attn, first_attn, second_attn = adam_half(plan, attn, 1, [attn_y, cross_y], attn_states, near_done)
    return (
        activations,
        input_grad,
        new_attn,
        first_attn,
        second_attn,
        new_mlp,
        first_mlp,
        second_mlp,
        new_vec,
        first_vec,
        second_vec,
    )


def solution(mesh):
    rows, both = P("opt", None), P(("dp", "opt"), None)
    in_specs = (both, P(("dp", "opt")), both) + (rows,) * 6 + (P("opt"),) * 3
    out_specs = (both, both) + (rows,) * 6 + (P("opt"),) * 3
    return jax.shard_map(
        functools.partial(body, Plan(mesh)), mesh=mesh, in_specs=in_specs, out_specs=out_specs, check_vma=False
    )
```
